32 devices in a mesh: section: 4 (over y, x), dp: 8 (over z, core).
Axes of the slice: x: 2, y: 2, z: 4, core: 2. Of those that a mesh axis runs over, the one named last changes fastest.
Arguments:
- tokens: bfloat16 [4, 8, 196, 256], P('section', 'dp'), may hold values from -6 to 6
- routes: int32 [4, 8, 2, 8, 49, 4], P('section', 'dp'), may hold values from 0 to 48, all different within a row
- pos_weight: bfloat16 [2, 9, 256], replicated, may hold values from -2 to 2
- attn_gain: bfloat16 [2, 256], replicated, may hold values from 0.5 to 1.5
- attn_bias: bfloat16 [2, 256], replicated, may hold values from -3 to 3
- qkv_weight: bfloat16 [2, 256, 768], replicated, may hold values from -0.375 to 0.375
- lepe_weight: bfloat16 [2, 25, 256], replicated, may hold values from -1.25 to 1.25
- proj_weight: bfloat16 [2, 256, 256], replicated, may hold values from -0.375 to 0.375
- mlp_gain: bfloat16 [2, 256], replicated, may hold values from 0.5 to 1.5
- mlp_bias: bfloat16 [2, 256], replicated, may hold values from -3 to 3
- fc1_weight: bfloat16 [2, 256, 768], replicated, may hold values from -0.375 to 0.375
- fc2_weight: bfloat16 [2, 768, 256], replicated, may hold values from -0.21875 to 0.21875
- cotangent: bfloat16 [4, 8, 196, 256], P('section', 'dp'), may hold values from -6 to 6
Outputs:
- block_output: bfloat16 [4, 8, 196, 256], P('section', 'dp')
- input_grad: bfloat16 [4, 8, 196, 256], P('section', 'dp')
- pos_grad: float32 [2, 9, 256], replicated
- attn_gain_grad: float32 [2, 256], replicated
- attn_bias_grad: float32 [2, 256], replicated
- qkv_grad: float32 [2, 256, 768], replicated
- lepe_grad: float32 [2, 25, 256], replicated
- proj_grad: float32 [2, 256, 256], replicated
- mlp_gain_grad: float32 [2, 256], replicated
- mlp_bias_grad: float32 [2, 256], replicated
- fc1_grad: float32 [2, 256, 768], replicated
- fc2_grad: float32 [2, 768, 256], replicated
The draws below stay inside these ranges and needn't reach their ends.
Inputs may be any that keep to these rules, and one draw needn't show every extreme that they name: `routes`: each row of 4 names different regions.
All inputs are finite; a program needn't handle non-finite values.
Results may differ from the reference program's by a relative error of at most 0.018.
Values may be sent and summed in bfloat16 or wider, within the bound.
A program may use at most 320 MiB of HBM per device.

```python
import math
import jax
import jax.numpy as jnp
from jax import lax

D = 256
HEADS = 8
FF = 768
SIDE = 14
REG_SIDE = 7
TOPK = 4
LAYERS = 2
HEAD_DIM = 32
TOK_IMG = 196
REGIONS = 49
MB = 4
IMG_GROUP = 8


def steps_of(key, dims, split, low, high):
    def one(dim, blocks):
        heights = jax.random.uniform(jax.random.fold_in(jax.random.fold_in(key, 6), dim), (blocks,), jnp.float32, low / len(split), high / len(split))
        return jnp.repeat(jnp.exp(heights), dims[dim] // blocks).reshape((-1,) + (1,) * (len(dims) - dim - 1))

    level = one(*split[0])
    for cut in split[1:]:
        level = level * one(*cut)
    return level


def different_ones(own_key, rows, count, top, lift):
    sequence = jax.random.permutation(jax.random.fold_in(own_key, 1), count)
    favour = sequence
    for power in range(3):
        favour = favour * favour // count
    favour = favour * lift // count
    chance = jax.random.randint(jax.random.fold_in(own_key, 2), (rows, count), 0, 4096) + favour
    fixed_rows = jax.random.permutation(jax.random.fold_in(own_key, 3), rows)[jnp.arange(count) % rows]
    chance = jnp.where(jnp.arange(rows)[:, None] == fixed_rows[None, :], 1 << 14, chance)
    priority = chance * count + jnp.arange(count)
    return lax.top_k(priority.astype(jnp.int32), top)[1].astype(jnp.int32)


def centred(rng, shape, deviation, most, pieces=(), held_as=jnp.bfloat16):
    level = steps_of(rng, shape, pieces, -0.22, 0.18) if pieces else 1.0
    drawn = jax.random.normal(rng, shape, jnp.float32) * deviation * level
    return jnp.minimum(jnp.maximum(drawn, -most), most).astype(held_as)


def setup_inputs(seed: int = 0) -> dict:
    streams_of = jax.random.split(jax.random.key(seed), 14)
    tokens = centred(streams_of[0], (MB, IMG_GROUP, TOK_IMG, D), 1.0, 6.0, ((0, 4), (1, 8)))
    routes = different_ones(streams_of[1], MB * IMG_GROUP * LAYERS * HEADS * REGIONS, REGIONS, TOPK, 1337).reshape((MB, IMG_GROUP, LAYERS, HEADS, REGIONS, TOPK))
    pos_weight = centred(streams_of[2], (LAYERS, 9, D), 9 ** -0.5, 2.0)
    attn_gain = jnp.clip(1.0 + 0.1 * jax.random.normal(streams_of[3], (LAYERS, D), jnp.float32), 0.5, 1.5).astype(jnp.bfloat16)
    attn_bias = centred(streams_of[4], (LAYERS, D), 0.3, 3.0)
    qkv_weight = centred(streams_of[5], (LAYERS, D, 3 * D), D ** -0.5, 0.375)
    lepe_weight = centred(streams_of[6], (LAYERS, 25, D), 25 ** -0.5, 1.25)
    proj_weight = centred(streams_of[7], (LAYERS, D, D), D ** -0.5, 0.375)
    mlp_gain = jnp.clip(1.0 + 0.1 * jax.random.normal(streams_of[8], (LAYERS, D), jnp.float32), 0.5, 1.5).astype(jnp.bfloat16)
    mlp_bias = centred(streams_of[9], (LAYERS, D), 0.3, 3.0)
    fc1_weight = centred(streams_of[10], (LAYERS, D, FF), D ** -0.5, 0.375)
    fc2_weight = centred(streams_of[11], (LAYERS, FF, D), FF ** -0.5, 0.21875)
    cotangent = centred(streams_of[12], (MB, IMG_GROUP, TOK_IMG, D), 1.0, 6.0, ((0, 4), (1, 8)))
    return {"tokens": tokens, "routes": routes, "pos_weight": pos_weight, "attn_gain": attn_gain, "attn_bias": attn_bias, "qkv_weight": qkv_weight, "lepe_weight": lepe_weight, "proj_weight": proj_weight, "mlp_gain": mlp_gain, "mlp_bias": mlp_bias, "fc1_weight": fc1_weight, "fc2_weight": fc2_weight, "cotangent": cotangent}


@jax.custom_vjp
def low(v):
    return lax.optimization_barrier(v.astype(jnp.bfloat16)).astype(jnp.float32)

@jax.custom_vjp
def low_back(v):
    return v

def low_keep(v):
    return (low(v), None)

def low_pass(kept, grad):
    return (grad,)

def back_keep(v):
    return (v, None)

def back_low(kept, grad):
    return (low(grad),)
low.defvjp(low_keep, low_pass)
low_back.defvjp(back_keep, back_low)
EPS = 1e-06
HIGH = lax.Precision.HIGHEST

def depthwise(signal, kernel):
    images = signal.shape[0]
    channels = signal.shape[-1]
    extent = math.isqrt(kernel.shape[0])
    radius = extent // 2
    picture = signal.reshape(images, SIDE, SIDE, channels)
    padded = jnp.pad(picture, ((0, 0), (radius, radius), (radius, radius), (0, 0)))
    summed = jnp.zeros_like(picture)
    for row_tap in range(extent):
        for col_tap in range(extent):
            summed = summed + padded[:, row_tap:row_tap + SIDE, col_tap:col_tap + SIDE, :] * kernel[row_tap * extent + col_tap]
    return summed.reshape(images, SIDE * SIDE, channels)

def norm_rows(signal, gain, bias):
    average = lax.optimization_barrier(jnp.mean(signal, axis=-1, keepdims=True))
    centered = signal - average
    variance = lax.optimization_barrier(jnp.mean(centered * centered, axis=-1, keepdims=True))
    return centered * lax.rsqrt(variance + EPS) * gain + bias

def to_regions(signal):
    images = signal.shape[0]
    channels = signal.shape[-1]
    patch_side = SIDE // REG_SIDE
    grid = signal.reshape(images, REG_SIDE, patch_side, REG_SIDE, patch_side, channels)
    return grid.transpose(0, 1, 3, 2, 4, 5).reshape(images, REG_SIDE * REG_SIDE, patch_side * patch_side, channels)

def from_regions(signal):
    images = signal.shape[0]
    channels = signal.shape[-1]
    patch_side = SIDE // REG_SIDE
    grid = signal.reshape(images, REG_SIDE, REG_SIDE, patch_side, patch_side, channels)
    return grid.transpose(0, 1, 3, 2, 4, 5).reshape(images, SIDE * SIDE, channels)

def heads_of(signal):
    regional = to_regions(signal)
    images, region_count, inside, channels = regional.shape
    return regional.reshape(images, region_count, inside, HEADS, channels // HEADS).transpose(0, 3, 1, 2, 4)

def merge_heads(signal):
    images, head_count, region_count, inside, head_width = signal.shape
    return from_regions(signal.transpose(0, 2, 3, 1, 4).reshape(images, region_count, inside, head_count * head_width))

def gather_regions(onehot, signal):
    grouped = heads_of(signal)
    images, head_count, region_count, inside, head_width = grouped.shape
    grouped = grouped.reshape(images, head_count, region_count, inside * head_width)
    picked = jnp.einsum('ihrjs,ihsm->ihrjm', onehot, grouped, precision=HIGH)
    return picked.reshape(images, head_count, region_count, TOPK * inside, head_width)

def attention(signal, routed, pos_w, gain, bias, qkv_w, lepe_w, proj_w):
    features = signal.shape[-1]
    mixed_in = signal + depthwise(signal, pos_w)
    normed = low_back(low(norm_rows(mixed_in, gain, bias)))
    packed = low_back(low(jnp.einsum('itd,de->ite', normed, qkv_w, precision=HIGH)))
    queries = packed[..., :features]
    keys_tok = packed[..., features:2 * features]
    values_tok = packed[..., 2 * features:]
    onehot = (routed[..., None] == jnp.arange(REGIONS, dtype=jnp.int32)).astype(jnp.float32)
    picked_keys = low_back(gather_regions(onehot, keys_tok))
    picked_values = low_back(gather_regions(onehot, values_tok))
    query_heads = heads_of(queries)
    scores = low_back(jnp.einsum('ihrqc,ihrkc->ihrqk', query_heads, picked_keys, precision=HIGH) * HEAD_DIM ** (-0.5))
    attn_probs = low(jax.nn.softmax(scores, axis=-1))
    attended = jnp.einsum('ihrqk,ihrkc->ihrqc', attn_probs, picked_values, precision=HIGH)
    context = low_back(low(merge_heads(attended) + depthwise(values_tok, lepe_w)))
    return mixed_in + jnp.einsum('itd,de->ite', context, proj_w, precision=HIGH)

def feed_forward(signal, gain, bias, fc1_w, fc2_w):
    normed = low_back(low(norm_rows(signal, gain, bias)))
    hidden = low_back(jnp.einsum('itd,df->itf', normed, fc1_w, precision=HIGH))
    active = low_back(low(jax.nn.gelu(hidden, approximate=False)))
    return signal + jnp.einsum('itf,fd->itd', active, fc2_w, precision=HIGH)

def block(params, signal, routed):
    pos_w, a_gain, a_bias, qkv_w, lepe_w, proj_w, m_gain, m_bias, fc1_w, fc2_w = params
    for layer_index in range(LAYERS):
        signal = low_back(low(attention(signal, routed[:, layer_index], pos_w[layer_index], a_gain[layer_index], a_bias[layer_index], qkv_w[layer_index], lepe_w[layer_index], proj_w[layer_index])))
        signal = low_back(low(feed_forward(signal, m_gain[layer_index], m_bias[layer_index], fc1_w[layer_index], fc2_w[layer_index])))
    return signal

def reference(tokens, routes, pos_weight, attn_gain, attn_bias, qkv_weight, lepe_weight, proj_weight, mlp_gain, mlp_bias, fc1_weight, fc2_weight, cotangent):
    params = tuple((weight.astype(jnp.float32) for weight in (pos_weight, attn_gain, attn_bias, qkv_weight, lepe_weight, proj_weight, mlp_gain, mlp_bias, fc1_weight, fc2_weight)))
    image_count = MB * IMG_GROUP
    group_size = math.gcd(image_count, 16)
    blocks_count = image_count // group_size
    signal = tokens.reshape(blocks_count, group_size, TOK_IMG, D).astype(jnp.float32)
    routed = routes.reshape(blocks_count, group_size, LAYERS, HEADS, REGIONS, TOPK)
    grads_in = cotangent.reshape(blocks_count, group_size, TOK_IMG, D).astype(jnp.float32)

    def scan_step(summed, inputs):
        part_signal, part_routes, part_grad = inputs
        result, pullback = jax.vjp(lambda weights, values: block(weights, values, part_routes), params, part_signal)
        weight_grads, signal_grad = pullback(part_grad)
        summed = jax.tree.map(jnp.add, summed, weight_grads)
        return (summed, (result, signal_grad))
    zeros_init = jax.tree.map(jnp.zeros_like, params)
    summed, (outputs, input_grads) = lax.scan(scan_step, zeros_init, (signal, routed, grads_in))
    out_shape = (MB, IMG_GROUP, TOK_IMG, D)
    return (outputs.reshape(out_shape).astype(jnp.bfloat16), input_grads.reshape(out_shape).astype(jnp.bfloat16), summed[0], summed[1], summed[2], summed[3], summed[4], summed[5], summed[6], summed[7], summed[8], summed[9])
```

```python
from functools import partial
import math

import jax
import jax.numpy as jnp
from jax import lax
from jax.experimental import pallas as pl
from jax.experimental.pallas import tpu as pltpu
from jax.sharding import PartitionSpec as P

F32 = jnp.float32
BF16 = jnp.bfloat16
EPS = 1e-06
HEADS = 8
SIDE = 14
WIDE = 16
TOKS = SIDE * SIDE
ROWS = SIDE * WIDE
FULL = 256
D = 256
HD = 32
REGIONS = 49
TOPK = 4
BLOCKED = -1e30
LOG2E = 1.4426950408889634


def nn(a, b):
    return lax.dot_general(a, b, (((1,), (0,)), ((), ())), preferred_element_type=F32)


def nt(a, b):
    return lax.dot_general(a, b, (((1,), (1,)), ((), ())), preferred_element_type=F32)


def tn(a, b):
    return lax.dot_general(a, b, (((0,), (0,)), ((), ())), preferred_element_type=F32)


def iota(shape, dim):
    return lax.broadcasted_iota(jnp.int32, shape, dim)


def region_of(t):
    return (t >> 5) * (SIDE // 2) + ((t & 15) >> 1)


def valid(t):
    return ((t & 15) < SIDE) & (t < ROWS)


def keep_rows():
    return valid(iota((ROWS, 1), 0))


def norm_parts(v):
    mean = jnp.sum(v, axis=-1, keepdims=True) * (1.0 / D)
    cen = v - mean
    var = jnp.sum(cen * cen, axis=-1, keepdims=True) * (1.0 / D)
    rstd = lax.rsqrt(var + EPS)
    return cen * rstd, rstd


def shifted_into(s_ref, x, extent):
    radius = extent // 2
    for b in range(extent):
        away = b - radius
        s_ref[b, pl.ds(32, ROWS), :] = x if away == 0 else pltpu.roll(x, (-away) % ROWS, 0)


CH = 112


def conv_from(s_ref, taps, extent, flip, base, out_ref):
    radius = extent // 2
    for half in range(2):
        lanes = pl.ds(half * 128, 128)
        for c in range(ROWS // CH):
            acc = None
            for a in range(extent):
                for b in range(extent):
                    tap = a * extent + b
                    if flip:
                        tap = extent * extent - 1 - tap
                    part = s_ref[b, pl.ds(32 + c * CH + 16 * (a - radius), CH), lanes]
                    part = part * taps[pl.ds(tap, 1), lanes]
                    acc = part if acc is None else acc + part
            rows = pl.ds(c * CH, CH)
            if base is not None:
                acc = acc + base[rows, lanes]
            out_ref[rows, lanes] = acc


def conv_taps_grad(s_ref, d_ref, extent, store):
    radius = extent // 2
    for half in range(2):
        lanes = pl.ds(half * 128, 128)
        sums = [None] * (extent * extent)
        for c in range(ROWS // CH):
            d = d_ref[pl.ds(c * CH, CH), lanes]
            for a in range(extent):
                for b in range(extent):
                    part = s_ref[b, pl.ds(32 + c * CH + 16 * (a - radius), CH), lanes] * d
                    part = jnp.sum(part.reshape(CH // 8, 8, 128), axis=0)
                    tap = a * extent + b
                    sums[tap] = part if sums[tap] is None else sums[tap] + part
        for tap, s in enumerate(sums):
            store(tap, lanes, jnp.sum(s, axis=0, keepdims=True))


def half_lanes_mask(h):
    lane = iota((1, 128), 1)
    lo = (h % 4) * HD
    return (lane >= lo) & (lane < lo + HD)


def gelu_pair(x):
    cdf = 0.5 * (1.0 + lax.erf(x * (2.0**-0.5)))
    pdf = jnp.exp2(x * x * (-0.5 * LOG2E)) * (1.0 / math.sqrt(2.0 * math.pi))
    return x * cdf, cdf + x * pdf


class K:
    pass


def attn_fwd(l, k):
    x = k.x[...]
    shifted_into(k.sx.at[l], x, 3)
    conv_from(k.sx.at[l], k.posf.at[l], 3, False, k.x, k.tmp)
    mixed = k.tmp[...]
    xhat, rstd = norm_parts(mixed)
    k.a_xhat[l] = xhat
    k.a_rstd[l] = rstd
    gain = k.againf[pl.ds(l, 1), :]
    bias = k.abiasf[pl.ds(l, 1), :]
    normed = jnp.where(keep_rows(), xhat * gain + bias, 0.0).astype(BF16)
    k.a_normed[l] = normed
    packed = nn(normed, k.qkv[l]).astype(BF16)
    q = packed[:, :D]
    key = packed[:, D : 2 * D]
    val = packed[:, 2 * D :]
    k.key[l] = key
    k.val[l] = val
    zpad = jnp.zeros((FULL - ROWS, D), BF16)
    k.qT[l] = jnp.concatenate([q, zpad], 0).T
    k.kT[l] = jnp.concatenate([key, zpad], 0).T
    k.vT[l] = jnp.concatenate([val, zpad], 0).T
    shifted_into(k.sv.at[l], val.astype(F32), 5)
    conv_from(k.sv.at[l], k.lepef.at[l], 5, False, None, k.tmp2)
    ekey = k.ekey[...]
    eqT = k.eqT[...]
    c = HD**-0.5 * LOG2E
    for half in range(2):
        lanes = slice(half * 128, half * 128 + 128)
        rhs = jnp.concatenate([k.qT[l, lanes, :], eqT], 0)
        khalf = k.key[l, :, lanes]
        for hh in range(4):
            h = half * 4 + hh
            blocked = nn(ekey, k.open[l * HEADS + h]).astype(BF16)
            lhs = jnp.concatenate([jnp.where(half_lanes_mask(h), khalf, jnp.zeros_like(khalf)), blocked], 1)
            s = nn(lhs, rhs)
            m = jnp.max(s, axis=0, keepdims=True)
            e = jnp.exp2((s - m) * c)
            r = 1.0 / jnp.sum(e, axis=0, keepdims=True)
            p = e * r
            k.p[l * HEADS + h] = p
            pb = p.astype(BF16)
            k.pb[l * HEADS + h, :ROWS] = pb
            k.oT[pl.ds(h * HD, HD), :] = nn(k.vT[l, pl.ds(h * HD, HD), :], k.pb[l * HEADS + h])
    ctx = (k.oT[...].T[:ROWS] + k.tmp2[...]).astype(BF16)
    k.ctx[l] = ctx
    res = k.tmp[...] + nn(ctx, k.proj[l])
    k.x[...] = jnp.where(keep_rows(), res, 0.0).astype(BF16).astype(F32)


def mlp_fwd(l, k):
    x = k.x[...]
    xhat, rstd = norm_parts(x)
    k.m_xhat[l] = xhat
    k.m_rstd[l] = rstd
    normed = (xhat * k.mgainf[pl.ds(l, 1), :] + k.mbiasf[pl.ds(l, 1), :]).astype(BF16)
    k.m_normed[l] = normed
    hidden = nn(normed, k.fc1[l])
    act, slope = gelu_pair(hidden)
    act = act.astype(BF16)
    k.act[l] = act
    k.slope[l] = slope
    res = x + nn(act, k.fc2[l])
    k.x[...] = jnp.where(keep_rows(), res, 0.0).astype(BF16).astype(F32)


def norm_bwd(dy, xhat, rstd, gain, store_gain, store_bias):
    store_gain(jnp.sum(dy * xhat, axis=0, keepdims=True))
    store_bias(jnp.sum(dy, axis=0, keepdims=True))
    dg = dy * gain
    m1 = jnp.sum(dg, axis=-1, keepdims=True) * (1.0 / D)
    m2 = jnp.sum(dg * xhat, axis=-1, keepdims=True) * (1.0 / D)
    return rstd * (dg - m1 - xhat * m2)


def mlp_bwd(l, k):
    g = k.g[...]
    gb = g.astype(BF16)
    k.store("fc2", l, tn(k.act[l], gb))
    dact = nt(gb, k.fc2[l]).astype(BF16).astype(F32)
    dhid = (k.slope[l] * dact).astype(BF16)
    k.store("fc1", l, tn(k.m_normed[l], dhid))
    dn = nt(dhid, k.fc1[l]).astype(BF16).astype(F32)
    dx = norm_bwd(
        dn,
        k.m_xhat[l],
        k.m_rstd[l],
        k.mgainf[pl.ds(l, 1), :],
        lambda v: k.store_row("mgain", l, 0, slice(None), v),
        lambda v: k.store_row("mbias", l, 0, slice(None), v),
    )
    k.g[...] = (dx + g).astype(BF16).astype(F32)


def attn_bwd_start(l, k):
    g = k.g[...]
    gb = g.astype(BF16)
    k.store("proj", l, tn(k.ctx[l], gb))
    dctx = nt(gb, k.proj[l]).astype(BF16)
    dctx32 = dctx.astype(F32)
    k.tmp[...] = dctx32
    zpad = jnp.zeros((FULL - ROWS, D), BF16)
    k.dcT[...] = jnp.concatenate([dctx, zpad], 0).T
    shifted_into(k.sd, dctx32, 5)


def attn_bwd_lepe(l, k):
    conv_taps_grad(k.sv.at[l], k.tmp, 5, lambda tap, lanes, v: k.store_row("lepe", l, tap, lanes, v))


def attn_bwd_conv(l, k):
    conv_from(k.sd, k.lepef.at[l], 5, True, None, k.tmp2)


def attn_bwd_heads(l, k, half):
    scale = HD**-0.5
    lanes = slice(half * 128, half * 128 + 128)
    vhalf = k.val[l, :, lanes]
    rhs = k.dcT[lanes, :]
    for hh in range(4):
        h = half * 4 + hh
        hrows = pl.ds(h * HD, HD)
        dp = nn(jnp.where(half_lanes_mask(h), vhalf, jnp.zeros_like(vhalf)), rhs)
        k.dvT[hrows, :] = nt(k.dcT[hrows, :], k.pb[l * HEADS + h])
        p = k.p[l * HEADS + h]
        pd = p * dp
        ds = pd - p * jnp.sum(pd, axis=0, keepdims=True)
        k.ds[hh % 2, :ROWS] = ds.astype(BF16)
        dsb = k.ds[hh % 2]
        k.dqT[hrows, :] = nn(k.kT[l, hrows, :], dsb) * scale
        k.dkT[hrows, :] = nt(k.qT[l, hrows, :], dsb) * scale
    dq = k.dqT[lanes, :].T[:ROWS].astype(BF16)
    dk = k.dkT[lanes, :].T[:ROWS].astype(BF16)
    dv = jnp.where(keep_rows(), k.dvT[lanes, :].T[:ROWS] + k.tmp2[:, lanes], 0.0).astype(BF16)
    k.dpacked[:, lanes] = dq
    k.dpacked[:, slice(D + half * 128, D + half * 128 + 128)] = dk
    k.dpacked[:, slice(2 * D + half * 128, 2 * D + half * 128 + 128)] = dv
    k.store("qkv%d" % half, l, tn(k.a_normed[l], jnp.concatenate([dq, dk, dv], 1)))


def attn_bwd_end(l, k):
    g = k.g[...]
    dn = nt(k.dpacked[...], k.qkv[l]).astype(BF16).astype(F32)
    dx = norm_bwd(
        dn,
        k.a_xhat[l],
        k.a_rstd[l],
        k.againf[pl.ds(l, 1), :],
        lambda v: k.store_row("again", l, 0, slice(None), v),
        lambda v: k.store_row("abias", l, 0, slice(None), v),
    )
    dmixed = dx + g
    k.tmp[...] = dmixed
    conv_taps_grad(k.sx.at[l], k.tmp, 3, lambda tap, lanes, v: k.store_row("pos", l, tap, lanes, v))


def attn_bwd_input(l, k):
    dmixed = k.tmp[...]
    shifted_into(k.sd, dmixed, 3)
    conv_from(k.sd, k.posf.at[l], 3, True, k.tmp, k.tmp2)
    k.g[...] = jnp.where(keep_rows(), k.tmp2[...], 0.0).astype(BF16).astype(F32)


def prepare(k, tok, cot, routes):
    t = iota((ROWS, TOKS), 0)
    spread = ((t >> 4) * SIDE + (t & 15) == iota((ROWS, TOKS), 1)) & valid(t)
    spread = spread.astype(F32).astype(BF16)
    k.x[...] = nn(spread, tok)
    k.g[...] = nn(spread, cot)
    t = iota((ROWS, 128), 0)
    reg = jnp.where(valid(t), region_of(t), REGIONS)
    k.ekey[...] = (reg == iota((ROWS, 128), 1)).astype(F32).astype(BF16)
    t = iota((128, FULL), 1)
    k.eqT[...] = ((region_of(t) == iota((128, FULL), 0)) & valid(t)).astype(F32).astype(BF16)
    place = iota((128, REGIONS), 0)
    k.open[...] = jnp.zeros_like(k.open)
    k.pb[:, ROWS:, :] = jnp.zeros((k.pb.shape[0], FULL - ROWS, FULL), BF16)
    k.ds[:, ROWS:, :] = jnp.zeros((2, FULL - ROWS, FULL), BF16)
    for ref in (k.sx, k.sv):
        for l in range(ref.shape[0]):
            for b in range(ref.shape[1]):
                ref[l, b, :32] = jnp.zeros((32, D), F32)
                ref[l, b, 32 + ROWS :] = jnp.zeros((32, D), F32)
    for b in range(5):
        k.sd[b, :32] = jnp.zeros((32, D), F32)
        k.sd[b, 32 + ROWS :] = jnp.zeros((32, D), F32)
    for lh in range(k.open.shape[0]):
        hit = None
        for j in range(TOPK):
            same = routes[lh // HEADS, lh % HEADS, pl.ds(j, 1), :] == place
            hit = same if hit is None else hit | same
        k.open[lh, :, :REGIONS] = jnp.where(hit, 0.0, BLOCKED).astype(BF16)
    k.againf[:k.again.shape[0], :] = k.again[...].astype(F32)
    k.abiasf[:k.abias.shape[0], :] = k.abias[...].astype(F32)
    k.mgainf[:k.mgain.shape[0], :] = k.mgain[...].astype(F32)
    k.mbiasf[:k.mbias.shape[0], :] = k.mbias[...].astype(F32)
    for tap in range(9):
        k.posf[:, tap, :] = k.pos[tap].astype(F32)
    for tap in range(25):
        k.lepef[:, tap, :] = k.lepe[tap].astype(F32)


def scratch(layers):
    one = pltpu.VMEM
    return dict(
        againf=one((8, D), F32),
        abiasf=one((8, D), F32),
        mgainf=one((8, D), F32),
        mbiasf=one((8, D), F32),
        posf=one((layers, 16, D), F32),
        lepef=one((layers, 32, D), F32),
        x=one((ROWS, D), F32),
        g=one((ROWS, D), F32),
        tmp=one((ROWS, D), F32),
        tmp2=one((ROWS, D), F32),
        sx=one((layers, 3, 64 + ROWS, D), F32),
        sv=one((layers, 5, 64 + ROWS, D), F32),
        sd=one((5, 64 + ROWS, D), F32),
        a_xhat=one((layers, ROWS, D), F32),
        a_rstd=one((layers, ROWS, 1), F32),
        a_normed=one((layers, ROWS, D), BF16),
        key=one((layers, ROWS, D), BF16),
        val=one((layers, ROWS, D), BF16),
        qT=one((layers, D, FULL), BF16),
        kT=one((layers, D, FULL), BF16),
        vT=one((layers, D, FULL), BF16),
        oT=one((D, FULL), F32),
        dcT=one((D, FULL), BF16),
        dqT=one((D, FULL), F32),
        dkT=one((D, FULL), F32),
        dvT=one((D, FULL), F32),
        dpacked=one((ROWS, 3 * D), BF16),
        p=one((layers * HEADS, ROWS, FULL), F32),
        pb=one((layers * HEADS, FULL, FULL), BF16),
        ds=one((2, FULL, FULL), BF16),
        open=one((layers * HEADS, 128, 128), BF16),
        ekey=one((ROWS, 128), BF16),
        eqT=one((128, FULL), BF16),
        ctx=one((layers, ROWS, D), BF16),
        m_xhat=one((layers, ROWS, D), F32),
        m_rstd=one((layers, ROWS, 1), F32),
        m_normed=one((layers, ROWS, D), BF16),
        act=one((layers, ROWS, 3 * D), BF16),
        slope=one((layers, ROWS, 3 * D), F32),
    )


class Group:
    def __init__(self, where, axis, stride, size):
        self.where, self.axis, self.stride, self.size = where, axis, stride, size
        self.index = (where[axis] // stride) % size

    def member(self, j):
        at = list(self.where)
        at[self.axis] = self.where[self.axis] + (j - self.index) * self.stride
        return tuple(at)

    def after(self, step):
        return lax.rem(self.index + step, self.size)


class Exchange:
    def __init__(self, mine, total, base, rows, groups, bufs, send, recv):
        self.mine, self.total, self.groups = mine, total, groups
        self.bufs, self.send, self.recv = bufs, send, recv
        self.base, self.rows = [base], [rows]
        for group, split in groups:
            size = self.rows[-1] // group.size if split else self.rows[-1]
            self.rows.append(size)
            self.base.append(self.base[-1] + group.index * size if split else self.base[-1])
        self.flight = None

    def part(self, stage, j):
        size = self.rows[stage + 1]
        return pl.ds(pl.multiple_of(self.base[stage] + j * size, 16), size)

    def own(self, stage):
        return pl.ds(pl.multiple_of(self.base[stage], 16), self.rows[stage])

    def copy(self, sem, src, dst, to):
        return pltpu.make_async_remote_copy(
            src_ref=src,
            dst_ref=dst,
            send_sem=self.send.at[sem],
            recv_sem=self.recv.at[sem],
            device_id=to,
            device_id_type=pl.DeviceIdType.MESH,
        )

    def go(self, stage):
        group, split = self.groups[stage]
        sem, buf = self.bufs[stage]
        self.flight = []
        if not split:
            buf[group.index] = self.mine[self.own(stage), :]
        for step in range(1, group.size):
            to = group.after(step)
            if split:
                src, dst = self.mine.at[self.part(stage, to), :], buf.at[step - 1]
            else:
                src, dst = self.mine.at[self.own(stage), :], buf.at[group.index]
            copy = self.copy(sem + step - 1, src, dst, group.member(to))
            copy.start()
            if not split:
                came = lax.rem(group.index + group.size - step, group.size)
                copy = (copy, self.copy(sem + step - 1, src, buf.at[came], group.member(to)))
            else:
                copy = (copy, copy)
            self.flight.append(copy)

    def add(self, stage):
        group, split = self.groups[stage]
        _, buf = self.bufs[stage]
        for out, into in self.flight:
            out.wait_send()
            into.wait_recv()
        mine = self.own(stage + 1)
        last = stage + 1 == len(self.groups)
        to = self.total if last else self.mine
        if split:
            total = self.mine[mine, :].astype(F32)
            for step in range(group.size - 1):
                total = total + buf[step].astype(F32)
        else:
            total = buf[0].astype(F32)
            for j in range(1, group.size):
                total = total + buf[j].astype(F32)
        to[mine, :] = total.astype(BF16)

    def back(self, stage):
        group, split = self.groups[stage]
        self.flight = []
        if not split:
            return
        sem = self.bufs[stage][0] + group.size - 1
        rows = self.part(stage, group.index)
        for step in range(1, group.size):
            copy = self.copy(sem + step - 1, self.total.at[rows, :], self.total.at[rows, :], group.member(group.after(step)))
            copy.start()
            came = self.part(stage, lax.rem(group.index + group.size - step, group.size))
            into = self.copy(sem + step - 1, self.total.at[came, :], self.total.at[came, :], group.member(group.after(step)))
            self.flight.append((copy, into))

    def arrived(self):
        for out, into in self.flight:
            out.wait_send()
            into.wait_recv()

    def steps(self):
        last = len(self.groups) - 1
        for stage in range(last + 1):
            self.go(stage)
            yield
            self.add(stage)
        for stage in range(last, -1, -1):
            if self.groups[stage][1]:
                self.back(stage)
                yield
                self.arrived()


def groups_of(where, sections, dps):
    core = Group(where, 1, 1, 2)
    plane = Group(where, 0, 1, sections)
    far = min(4, dps // 2)
    line = Group(where, 1, 2, far)
    rest = dps // 2 // far
    more = [(Group(where, 1, 2 * far, rest), False)] if rest > 1 else []
    return core, plane, line, more


IN_NAMES = ("tok", "routes", "pos", "again", "abias", "qkv", "lepe", "proj", "mgain", "mbias", "fc1", "fc2", "cot")
G_NAMES = ("pos", "again", "abias", "qkv", "lepe", "proj", "mgain", "mbias", "fc1", "fc2")

SMALL = 128
LAST = 16


def row_map(layers):
    at, pieces, n = {}, [], 0
    for l in reversed(range(layers)):
        at["fc2", l], at["fc1", l] = n, n + 3 * D
        pieces.append((n, 6 * D))
        n += 6 * D
        start = n
        at["proj", l], at["qkv0", l] = n, n + D
        n += D + 384
        if l == 0:
            at["small"] = n
            n += SMALL
            pieces.append((start, n - start))
            start = n
        at["qkv1", l] = n
        n += 384
        pieces.append((start, n - start))
    at["last"] = n
    pieces.append((n, LAST))
    return at, pieces, n + LAST


def small_map(layers):
    at, n = {}, 0
    for l in reversed(range(layers)):
        names = (("pos", 9), ("again", 1), ("abias", 1), ("lepe", 25), ("mgain", 1), ("mbias", 1))
        for name, rows in names:
            if l == 0 and name in ("pos", "again", "abias"):
                continue
            at[name, l] = n
            n += rows
    assert n <= SMALL
    last = {("pos", 0): 0, ("again", 0): 9, ("abias", 0): 10}
    return at, last


def plan(where, sections, dps, layers):
    core, plane, line, more = groups_of(where, sections, dps)
    _, pieces, _ = row_map(layers)
    plans = []
    for n, (base, rows) in enumerate(pieces):
        shares = rows // 16
        groups = []
        for group in (core, plane, line):
            split = shares % group.size == 0
            if split:
                shares //= group.size
            groups.append((group, split))
        plans.append((base, rows, groups + more))
    return plans


def plan_buffers(plans):
    shapes, sems = [], 0
    where = []
    for base, rows, groups in plans:
        mine = []
        for group, split in groups:
            if split:
                rows //= group.size
                shapes.append(pltpu.VMEM((group.size - 1, rows, D), BF16))
                mine.append((sems, len(shapes) - 1))
                sems += 2 * (group.size - 1)
            else:
                shapes.append(pltpu.VMEM((group.size, rows, D), BF16))
                mine.append((sems, len(shapes) - 1))
                sems += group.size - 1
        where.append(mine)
    return shapes, sems, where


def body(layers, sections, dps, names, *refs):
    k = K()
    n_in = len(IN_NAMES)
    for name, ref in zip(IN_NAMES, refs[:n_in]):
        setattr(k, name, ref)
    out_ref, gin_ref, total = refs[n_in : n_in + 3]
    refs = refs[n_in + 3 :]
    for name, ref in zip(names, refs):
        setattr(k, name, ref)
    mine, small, last, send, recv = refs[len(names) : len(names) + 5]
    bufs = refs[len(names) + 5 :]

    where = (lax.axis_index("section"), lax.axis_index("dp"))
    plans = plan(where, sections, dps, layers)
    _, _, slots = plan_buffers(plans)
    barrier = pltpu.get_barrier_semaphore()
    partners = 0
    for group, _ in plans[0][2]:
        for step in range(1, group.size):
            pl.semaphore_signal(barrier, inc=1, device_id=group.member(group.after(step)), device_id_type=pl.DeviceIdType.MESH)
            partners += 1

    at, pieces, _ = row_map(layers)
    small_at, last_at = small_map(layers)

    def store(name, l, v):
        n = at[name, l]
        v = v.astype(BF16)
        if name == "fc1":
            for c in range(3):
                mine[pl.ds(n + c * D, D), :] = v[:, c * D : (c + 1) * D]
        elif name.startswith("qkv"):
            mine[pl.ds(n, D), :] = v[:, :D]
            mine[pl.ds(n + D, 128), :128] = v[:128, D:]
            mine[pl.ds(n + D, 128), 128:] = v[128:, D:]
        else:
            mine[pl.ds(n, v.shape[0]), :] = v

    def store_row(name, l, tap, lanes, v):
        if (name, l) in small_at:
            small[pl.ds(small_at[name, l] + tap, 1), lanes] = v
        else:
            last[pl.ds(last_at[name, l] + tap, 1), lanes] = v

    k.store = store
    k.store_row = store_row
    small[...] = jnp.zeros_like(small)
    last[...] = jnp.zeros_like(last)
    prepare(k, k.tok[0, 0], k.cot[0, 0], k.routes.at[0, 0])

    def fwd(l, carry):
        attn_fwd(l, k)
        mlp_fwd(l, k)
        return carry

    lax.fori_loop(0, layers, fwd, 0)
    t = iota((TOKS, ROWS), 1)
    gathered = ((t >> 4) * SIDE + (t & 15) == iota((TOKS, ROWS), 0)) & valid(t)
    gathered = gathered.astype(F32).astype(BF16)
    out_ref[0, 0] = nn(gathered, k.x[...].astype(BF16)).astype(BF16)

    moves = []
    for (base, rows, groups), slot in zip(plans, slots):
        moves.append(
            Exchange(mine, total, base, rows, groups, [(sem, bufs[n]) for sem, n in slot], send, recv).steps()
        )

    def step(n):
        next(moves[n], None)

    for i in range(layers):
        l = layers - 1 - i
        first = i == 0
        mlp_bwd(l, k)
        if first:
            pl.semaphore_wait(barrier, partners)
            step(0)
            attn_bwd_start(l, k)
            step(0)
            attn_bwd_lepe(l, k)
            attn_bwd_conv(l, k)
            attn_bwd_heads(l, k, 0)
            attn_bwd_heads(l, k, 1)
            step(1)
            attn_bwd_end(l, k)
            step(1)
            attn_bwd_input(l, k)
            step(0)
        else:
            step(2)
            attn_bwd_start(l, k)
            step(2)
            step(1)
            attn_bwd_lepe(l, k)
            small_rows = pl.ds(at["small"], SMALL)
            mine[small_rows, :] = small[...].astype(BF16)
            attn_bwd_conv(l, k)
            step(0)
            attn_bwd_heads(l, k, 0)
            step(3)
            step(1)
            attn_bwd_heads(l, k, 1)
            step(4)
            step(3)
            step(0)
            step(2)
            attn_bwd_end(l, k)
            mine[pl.ds(at["last"], LAST), :] = last[...].astype(BF16)
            step(5)
            step(4)
            step(1)
            attn_bwd_input(l, k)
    gin_ref[0, 0] = nn(gathered, k.g[...].astype(BF16)).astype(BF16)
    live = list(moves)
    while live:
        for m in list(live):
            if next(m, live) is live:
                live.remove(m)


def finish_body(layers, total, out_in, gin_in, out, gin, pos, again, abias, qkv, lepe, proj, mgain, mbias, fc1, fc2):
    at, _, _ = row_map(layers)
    small_at, last_at = small_map(layers)
    out[...] = out_in[...]
    gin[...] = gin_in[...]
    small = total[pl.ds(at["small"], SMALL), :].astype(F32)
    last = total[pl.ds(at["last"], LAST), :].astype(F32)

    def rows_of(name, l, count):
        if (name, l) in small_at:
            n = small_at[name, l]
            return small[n : n + count]
        n = last_at[name, l]
        return last[n : n + count]

    for l in range(layers):
        for name, ref, count in (("pos", pos, 9), ("lepe", lepe, 25)):
            rows = rows_of(name, l, count)
            for tap in range(count):
                ref[tap, pl.ds(l, 1), :] = rows[tap : tap + 1]
        for name, ref in (("again", again), ("abias", abias), ("mgain", mgain), ("mbias", mbias)):
            ref[pl.ds(l, 1), :] = rows_of(name, l, 1)
        n = at["fc2", l]
        fc2[l] = total[pl.ds(n, 3 * D), :].astype(F32)
        n = at["fc1", l]
        for c in range(3):
            fc1[l, :, c * D : (c + 1) * D] = total[pl.ds(n + c * D, D), :].astype(F32)
        n = at["proj", l]
        proj[l] = total[pl.ds(n, D), :].astype(F32)
        for half in range(2):
            n = at["qkv%d" % half, l]
            both = total[pl.ds(n, D), :].astype(F32)
            lo = half * 128
            qkv[l, :, lo : lo + 128] = both[:, :128]
            qkv[l, :, D + lo : D + lo + 128] = both[:, 128:]
            tail = total[pl.ds(n + D, 128), :].astype(F32)
            qkv[l, :128, 2 * D + lo : 2 * D + lo + 128] = tail[:, :128]
            qkv[l, 128:, 2 * D + lo : 2 * D + lo + 128] = tail[:, 128:]


def per_device(sections, dps, tokens, routes, pos, again, abias, qkv, lepe, proj, mgain, mbias, fc1, fc2, cot):
    layers = pos.shape[0]
    assert tokens.shape == (1, 1, TOKS, D)
    sc = scratch(layers)
    pos_t, lepe_t = (jnp.transpose(a, (1, 0, 2)) for a in (pos, lepe))
    routes_t = jnp.swapaxes(routes, -1, -2)
    args = (tokens, routes_t, pos_t, again, abias, qkv, lepe_t, proj, mgain, mbias, fc1, fc2, cot)
    vm = pl.BlockSpec(memory_space=pltpu.VMEM)
    _, _, count = row_map(layers)
    shapes, sems, _ = plan_buffers(plan((0, 0), sections, dps, layers))
    params = pltpu.CompilerParams(vmem_limit_bytes=60 * 2**20, collective_id=0, has_side_effects=True)
    out, gin, total = pl.pallas_call(
        partial(body, layers, sections, dps, tuple(sc)),
        out_shape=[jax.ShapeDtypeStruct(tokens.shape, BF16)] * 2 + [jax.ShapeDtypeStruct((count, D), BF16)],
        in_specs=[vm] * len(args),
        out_specs=[vm] * 3,
        scratch_shapes=list(sc.values())
        + [
            pltpu.VMEM((count, D), BF16),
            pltpu.VMEM((SMALL, D), F32),
            pltpu.VMEM((LAST, D), F32),
            pltpu.SemaphoreType.DMA((sems,)),
            pltpu.SemaphoreType.DMA((sems,)),
        ]
        + shapes,
        compiler_params=params,
        name="blocks",
    )(*args)
    weights = (pos_t, again, abias, qkv, lepe_t, proj, mgain, mbias, fc1, fc2)
    res = pl.pallas_call(
        partial(finish_body, layers),
        out_shape=[jax.ShapeDtypeStruct(tokens.shape, BF16)] * 2 + [jax.ShapeDtypeStruct(w.shape, F32) for w in weights],
        in_specs=[vm] * 3,
        out_specs=[vm] * 12,
        compiler_params=pltpu.CompilerParams(vmem_limit_bytes=40 * 2**20),
        name="widen",
    )(total, out, gin)
    res = list(res)
    res[2] = jnp.transpose(res[2], (1, 0, 2))
    res[6] = jnp.transpose(res[6], (1, 0, 2))
    return tuple(res)


def solution(mesh):
    image = P("section", "dp", None, None)
    sections, dps = mesh.shape["section"], mesh.shape["dp"]
    return jax.shard_map(
        partial(per_device, sections, dps),
        mesh=mesh,
        in_specs=(image, P("section", "dp", None, None, None, None)) + (P(),) * 10 + (image,),
        out_specs=(image, image) + (P(),) * 10,
        check_vma=False,
    )
```

```python
from functools import partial
import math

import jax
import jax.numpy as jnp
from jax import lax
from jax.experimental import pallas as pl
from jax.experimental.pallas import tpu as pltpu
from jax.sharding import PartitionSpec as P

F32 = jnp.float32
BF16 = jnp.bfloat16
EPS = 1e-06
HEADS = 8
SIDE = 14
WIDE = 16
TOKS = SIDE * SIDE
ROWS = SIDE * WIDE
FULL = 256
D = 256
HD = 32
REGIONS = 49
TOPK = 4
BLOCKED = -1e30
LOG2E = 1.4426950408889634


def nn(a, b):
    return lax.dot_general(a, b, (((1,), (0,)), ((), ())), preferred_element_type=F32)


def nt(a, b):
    return lax.dot_general(a, b, (((1,), (1,)), ((), ())), preferred_element_type=F32)


def tn(a, b):
    return lax.dot_general(a, b, (((0,), (0,)), ((), ())), preferred_element_type=F32)


def iota(shape, dim):
    return lax.broadcasted_iota(jnp.int32, shape, dim)


def region_of(t):
    return (t >> 5) * (SIDE // 2) + ((t & 15) >> 1)


def valid(t):
    return ((t & 15) < SIDE) & (t < ROWS)


def keep_rows():
    return valid(iota((ROWS, 1), 0))


def norm_parts(v):
    mean = jnp.sum(v, axis=-1, keepdims=True) * (1.0 / D)
    cen = v - mean
    var = jnp.sum(cen * cen, axis=-1, keepdims=True) * (1.0 / D)
    rstd = lax.rsqrt(var + EPS)
    return cen * rstd, rstd


def shifted_into(s_ref, x, extent):
    radius = extent // 2
    for b in range(extent):
        away = b - radius
        s_ref[b, pl.ds(32, ROWS), :] = x if away == 0 else pltpu.roll(x, (-away) % ROWS, 0)


CH = 112


def conv_from(s_ref, taps, extent, flip, base, out_ref):
    radius = extent // 2
    for half in range(2):
        lanes = pl.ds(half * 128, 128)
        for c in range(ROWS // CH):
            acc = None
            for a in range(extent):
                for b in range(extent):
                    tap = a * extent + b
                    if flip:
                        tap = extent * extent - 1 - tap
                    part = s_ref[b, pl.ds(32 + c * CH + 16 * (a - radius), CH), lanes]
                    part = part * taps[pl.ds(tap, 1), lanes]
                    acc = part if acc is None else acc + part
            rows = pl.ds(c * CH, CH)
            if base is not None:
                acc = acc + base[rows, lanes]
            out_ref[rows, lanes] = acc


def conv_taps_grad(s_ref, d_ref, extent, store):
    radius = extent // 2
    for half in range(2):
        lanes = pl.ds(half * 128, 128)
        sums = [None] * (extent * extent)
        for c in range(ROWS // CH):
            d = d_ref[pl.ds(c * CH, CH), lanes]
            for a in range(extent):
                for b in range(extent):
                    part = s_ref[b, pl.ds(32 + c * CH + 16 * (a - radius), CH), lanes] * d
                    part = jnp.sum(part.reshape(CH // 8, 8, 128), axis=0)
                    tap = a * extent + b
                    sums[tap] = part if sums[tap] is None else sums[tap] + part
        for tap, s in enumerate(sums):
            store(tap, lanes, jnp.sum(s, axis=0, keepdims=True))


def head_keys(half):
    lane = iota((1, 128), 1)
    parts = []
    for hh in range(4):
        own = (lane >= hh * HD) & (lane < (hh + 1) * HD)
        parts.append(jnp.where(own, half, jnp.zeros_like(half)))
    return jnp.concatenate(parts, 0)


def gelu_pair(x):
    cdf = 0.5 * (1.0 + lax.erf(x * (2.0**-0.5)))
    pdf = jnp.exp2(x * x * (-0.5 * LOG2E)) * (1.0 / math.sqrt(2.0 * math.pi))
    return x * cdf, cdf + x * pdf


class K:
    pass


def attn_fwd(l, k):
    x = k.x[...]
    shifted_into(k.sx.at[l], x, 3)
    conv_from(k.sx.at[l], k.posf.at[l], 3, False, k.x, k.tmp)
    mixed = k.tmp[...]
    xhat, rstd = norm_parts(mixed)
    k.a_xhat[l] = xhat
    k.a_rstd[l] = rstd
    gain = k.againf[pl.ds(l, 1), :]
    bias = k.abiasf[pl.ds(l, 1), :]
    normed = jnp.where(keep_rows(), xhat * gain + bias, 0.0).astype(BF16)
    k.a_normed[l] = normed
    k.need(l, "qkv")
    packed = nn(normed, k.qkv[l]).astype(BF16)
    q = packed[:, :D]
    key = packed[:, D : 2 * D]
    val = packed[:, 2 * D :]
    k.key[l] = key
    k.val[l] = val
    zpad = jnp.zeros((FULL - ROWS, D), BF16)
    qT, kT, vT = (jnp.concatenate([part, zpad], 0).T for part in (q, key, val))
    k.qT[l] = qT
    k.kT[l] = kT
    shifted_into(k.sv.at[l], val.astype(F32), 5)
    conv_from(k.sv.at[l], k.lepef.at[l], 5, False, None, k.tmp2)
    eqT = k.eqT[...]
    c = HD**-0.5 * LOG2E
    zkeys = jnp.zeros((FULL - ROWS, FULL), BF16)
    outs = []
    for half in range(2):
        lanes = slice(half * 128, half * 128 + 128)
        heads = pl.ds(l * HEADS + half * 4, 4)
        rhs = jnp.concatenate([qT[lanes], eqT], 0)
        lhs = jnp.concatenate([head_keys(key[:, lanes]), k.blocked[heads].reshape(4 * ROWS, 128)], 1)
        s = nn(lhs, rhs).reshape(4, ROWS, FULL)
        m = jnp.max(s, axis=1, keepdims=True)
        e = jnp.exp2((s - m) * c)
        p = e * (1.0 / jnp.sum(e, axis=1, keepdims=True))
        k.p[heads] = p
        pb = p.astype(BF16)
        k.pb[heads, :ROWS] = pb
        for hh in range(4):
            h = half * 4 + hh
            outs.append(nn(vT[h * HD : (h + 1) * HD], jnp.concatenate([pb[hh], zkeys], 0)))
    ctx = (jnp.concatenate(outs, 0).T[:ROWS] + k.tmp2[...]).astype(BF16)
    k.ctx[l] = ctx
    k.need(l, "proj")
    res = k.tmp[...] + nn(ctx, k.proj[l])
    k.x[...] = jnp.where(keep_rows(), res, 0.0).astype(BF16).astype(F32)


def mlp_fwd(l, k):
    x = k.x[...]
    xhat, rstd = norm_parts(x)
    k.m_xhat[l] = xhat
    k.m_rstd[l] = rstd
    normed = (xhat * k.mgainf[pl.ds(l, 1), :] + k.mbiasf[pl.ds(l, 1), :]).astype(BF16)
    k.m_normed[l] = normed
    k.need(l, "fc1")
    hidden = nn(normed, k.fc1[l])
    act, slope = gelu_pair(hidden)
    act = act.astype(BF16)
    k.act[l] = act
    k.slope[l] = slope
    k.need(l, "fc2")
    res = x + nn(act, k.fc2[l])
    k.x[...] = jnp.where(keep_rows(), res, 0.0).astype(BF16).astype(F32)


def norm_bwd(dy, xhat, rstd, gain, store_gain, store_bias):
    store_gain(jnp.sum(dy * xhat, axis=0, keepdims=True))
    store_bias(jnp.sum(dy, axis=0, keepdims=True))
    dg = dy * gain
    m1 = jnp.sum(dg, axis=-1, keepdims=True) * (1.0 / D)
    m2 = jnp.sum(dg * xhat, axis=-1, keepdims=True) * (1.0 / D)
    return rstd * (dg - m1 - xhat * m2)


def mlp_bwd_fc2(l, k):
    k.store("fc2", l, tn(k.act[l], k.g[...].astype(BF16)))


def mlp_bwd(l, k):
    g = k.g[...]
    gb = g.astype(BF16)
    dact = nt(gb, k.fc2[l]).astype(BF16).astype(F32)
    dhid = (k.slope[l] * dact).astype(BF16)
    k.store("fc1", l, tn(k.m_normed[l], dhid))
    dn = nt(dhid, k.fc1[l]).astype(BF16).astype(F32)
    dx = norm_bwd(
        dn,
        k.m_xhat[l],
        k.m_rstd[l],
        k.mgainf[pl.ds(l, 1), :],
        lambda v: k.store_row("mgain", l, 0, slice(None), v),
        lambda v: k.store_row("mbias", l, 0, slice(None), v),
    )
    k.g[...] = (dx + g).astype(BF16).astype(F32)


def attn_bwd_start(l, k):
    g = k.g[...]
    gb = g.astype(BF16)
    k.store("proj", l, tn(k.ctx[l], gb))
    dctx = nt(gb, k.proj[l]).astype(BF16)
    dctx32 = dctx.astype(F32)
    k.dctx[l] = dctx32
    zpad = jnp.zeros((FULL - ROWS, D), BF16)
    k.dcT[...] = jnp.concatenate([dctx, zpad], 0).T
    shifted_into(k.sd, dctx32, 5)


def attn_bwd_lepe(l, k):
    conv_taps_grad(k.sv.at[l], k.dctx.at[l], 5, lambda tap, lanes, v: k.store_row("lepe", l, tap, lanes, v))


def attn_bwd_conv(l, k):
    conv_from(k.sd, k.lepef.at[l], 5, True, None, k.tmp2)


def attn_bwd_heads(l, k, half):
    scale = HD**-0.5
    lanes = slice(half * 128, half * 128 + 128)
    heads = pl.ds(l * HEADS + half * 4, 4)
    dcT = k.dcT[lanes]
    qT, kT = k.qT[l, lanes], k.kT[l, lanes]
    dp = nn(head_keys(k.val[l, :, lanes]), dcT).reshape(4, ROWS, FULL)
    p = k.p[heads]
    pb = k.pb[heads]
    pd = p * dp
    ds = (pd - p * jnp.sum(pd, axis=1, keepdims=True)).astype(BF16)
    zkeys = jnp.zeros((FULL - ROWS, FULL), BF16)
    dq, dk, dv = [], [], []
    for hh in range(4):
        rows = slice(hh * HD, (hh + 1) * HD)
        dsb = jnp.concatenate([ds[hh], zkeys], 0)
        dv.append(nt(dcT[rows], pb[hh]))
        dq.append(nn(kT[rows], dsb))
        dk.append(nt(qT[rows], dsb))
    dq, dk, dv = (jnp.concatenate(part, 0).T[:ROWS] for part in (dq, dk, dv))
    dq = (dq * scale).astype(BF16)
    dk = (dk * scale).astype(BF16)
    dv = jnp.where(keep_rows(), dv + k.tmp2[:, lanes], 0.0).astype(BF16)
    k.dpacked[:, lanes] = dq
    k.dpacked[:, slice(D + half * 128, D + half * 128 + 128)] = dk
    k.dpacked[:, slice(2 * D + half * 128, 2 * D + half * 128 + 128)] = dv
    k.store("qkv%d" % half, l, tn(k.a_normed[l], jnp.concatenate([dq, dk, dv], 1)))


def attn_bwd_end(l, k):
    g = k.g[...]
    dn = nt(k.dpacked[...], k.qkv[l]).astype(BF16).astype(F32)
    dx = norm_bwd(
        dn,
        k.a_xhat[l],
        k.a_rstd[l],
        k.againf[pl.ds(l, 1), :],
        lambda v: k.store_row("again", l, 0, slice(None), v),
        lambda v: k.store_row("abias", l, 0, slice(None), v),
    )
    dmixed = dx + g
    k.dmixed[l] = dmixed


def attn_bwd_pos(l, k):
    conv_taps_grad(k.sx.at[l], k.dmixed.at[l], 3, lambda tap, lanes, v: k.store_row("pos", l, tap, lanes, v))


def attn_bwd_input(l, k):
    shifted_into(k.sd, k.dmixed[l], 3)
    conv_from(k.sd, k.posf.at[l], 3, True, k.dmixed.at[l], k.tmp2)
    k.g[...] = jnp.where(keep_rows(), k.tmp2[...], 0.0).astype(BF16).astype(F32)


def prepare(k, tok, cot, routes):
    t = iota((ROWS, TOKS), 0)
    spread = ((t >> 4) * SIDE + (t & 15) == iota((ROWS, TOKS), 1)) & valid(t)
    spread = spread.astype(F32).astype(BF16)
    k.x[...] = nn(spread, tok)
    k.g[...] = nn(spread, cot)
    t = iota((ROWS, 128), 0)
    reg = jnp.where(valid(t), region_of(t), REGIONS)
    k.ekey[...] = (reg == iota((ROWS, 128), 1)).astype(F32).astype(BF16)
    t = iota((128, FULL), 1)
    k.eqT[...] = ((region_of(t) == iota((128, FULL), 0)) & valid(t)).astype(F32).astype(BF16)
    place = iota((128, REGIONS), 0)
    k.open[...] = jnp.zeros_like(k.open)
    k.pb[:, ROWS:, :] = jnp.zeros((k.pb.shape[0], FULL - ROWS, FULL), BF16)
    for ref in (k.sx, k.sv):
        for l in range(ref.shape[0]):
            for b in range(ref.shape[1]):
                ref[l, b, :32] = jnp.zeros((32, D), F32)
                ref[l, b, 32 + ROWS :] = jnp.zeros((32, D), F32)
    for b in range(5):
        k.sd[b, :32] = jnp.zeros((32, D), F32)
        k.sd[b, 32 + ROWS :] = jnp.zeros((32, D), F32)
    ekey = k.ekey[...]
    for lh in range(k.blocked.shape[0]):
        hit = None
        for j in range(TOPK):
            same = routes[lh // HEADS, lh % HEADS, pl.ds(j, 1), :] == place
            hit = same if hit is None else hit | same
        k.open[lh, :, :REGIONS] = jnp.where(hit, 0.0, BLOCKED).astype(BF16)
    for lh in range(0, k.blocked.shape[0], 2):
        both = nn(ekey, jnp.concatenate([k.open[lh], k.open[lh + 1]], 1)).astype(BF16)
        k.blocked[lh] = both[:, :128]
        k.blocked[lh + 1] = both[:, 128:]
    k.againf[:k.again.shape[0], :] = k.again[...].astype(F32)
    k.abiasf[:k.abias.shape[0], :] = k.abias[...].astype(F32)
    k.mgainf[:k.mgain.shape[0], :] = k.mgain[...].astype(F32)
    k.mbiasf[:k.mbias.shape[0], :] = k.mbias[...].astype(F32)
    for tap in range(9):
        k.posf[:, tap, :] = k.pos[tap].astype(F32)
    for tap in range(25):
        k.lepef[:, tap, :] = k.lepe[tap].astype(F32)


def scratch(layers):
    one = pltpu.VMEM
    return dict(
        againf=one((8, D), F32),
        abiasf=one((8, D), F32),
        mgainf=one((8, D), F32),
        mbiasf=one((8, D), F32),
        posf=one((layers, 16, D), F32),
        lepef=one((layers, 32, D), F32),
        x=one((ROWS, D), F32),
        g=one((ROWS, D), F32),
        tmp=one((ROWS, D), F32),
        tmp2=one((ROWS, D), F32),
        sx=one((layers, 3, 64 + ROWS, D), F32),
        sv=one((layers, 5, 64 + ROWS, D), F32),
        sd=one((5, 64 + ROWS, D), F32),
        a_xhat=one((layers, ROWS, D), F32),
        a_rstd=one((layers, ROWS, 1), F32),
        a_normed=one((layers, ROWS, D), BF16),
        key=one((layers, ROWS, D), BF16),
        val=one((layers, ROWS, D), BF16),
        qT=one((layers, D, FULL), BF16),
        kT=one((layers, D, FULL), BF16),
        dcT=one((D, FULL), BF16),
        dpacked=one((ROWS, 3 * D), BF16),
        dctx=one((layers, ROWS, D), F32),
        dmixed=one((layers, ROWS, D), F32),
        p=one((layers * HEADS, ROWS, FULL), F32),
        pb=one((layers * HEADS, FULL, FULL), BF16),
        blocked=one((layers * HEADS, ROWS, 128), BF16),
        open=one((layers * HEADS, 128, 128), BF16),
        ekey=one((ROWS, 128), BF16),
        eqT=one((128, FULL), BF16),
        ctx=one((layers, ROWS, D), BF16),
        m_xhat=one((layers, ROWS, D), F32),
        m_rstd=one((layers, ROWS, 1), F32),
        m_normed=one((layers, ROWS, D), BF16),
        act=one((layers, ROWS, 3 * D), BF16),
        slope=one((layers, ROWS, 3 * D), F32),
    )


class Group:
    def __init__(self, where, axis, stride, size, index=None):
        self.where, self.axis, self.stride, self.size = where, axis, stride, size
        self.index = (where[axis] // stride) % size if index is None else index

    def member(self, j):
        at = list(self.where)
        at[self.axis] = self.where[self.axis] + (j - self.index) * self.stride
        return tuple(at)

    def after(self, step):
        return lax.rem(self.index + step, self.size)


class Exchange:
    def __init__(self, mine, total, base, rows, groups, bufs, send, recv):
        self.mine, self.total, self.groups = mine, total, groups
        self.bufs, self.send, self.recv = bufs, send, recv
        self.base, self.rows = [base], [rows]
        for group, split in groups:
            size = self.rows[-1] // group.size if split else self.rows[-1]
            self.rows.append(size)
            self.base.append(self.base[-1] + group.index * size if split else self.base[-1])
        self.flight = None

    def part(self, stage, j):
        size = self.rows[stage + 1]
        return pl.ds(pl.multiple_of(self.base[stage] + j * size, 16), size)

    def own(self, stage):
        return pl.ds(pl.multiple_of(self.base[stage], 16), self.rows[stage])

    def copy(self, sem, src, dst, to):
        return pltpu.make_async_remote_copy(
            src_ref=src,
            dst_ref=dst,
            send_sem=self.send.at[sem],
            recv_sem=self.recv.at[sem],
            device_id=to,
            device_id_type=pl.DeviceIdType.MESH,
        )

    def go(self, stage):
        group, split = self.groups[stage]
        sem, buf = self.bufs[stage]
        self.flight = []
        if not split:
            buf[group.index] = self.mine[self.own(stage), :]
        for step in range(1, group.size):
            to = group.after(step)
            if split:
                src, dst = self.mine.at[self.part(stage, to), :], buf.at[step - 1]
            else:
                src, dst = self.mine.at[self.own(stage), :], buf.at[group.index]
            copy = self.copy(sem + step - 1, src, dst, group.member(to))
            copy.start()
            if not split:
                came = lax.rem(group.index + group.size - step, group.size)
                copy = (copy, self.copy(sem + step - 1, src, buf.at[came], group.member(to)))
            else:
                copy = (copy, copy)
            self.flight.append(copy)

    def add(self, stage):
        group, split = self.groups[stage]
        _, buf = self.bufs[stage]
        for out, into in self.flight:
            out.wait_send()
            into.wait_recv()
        mine = self.own(stage + 1)
        last = stage + 1 == len(self.groups)
        to = self.total if last else self.mine
        if split:
            total = self.mine[mine, :].astype(F32)
            for step in range(group.size - 1):
                total = total + buf[step].astype(F32)
        else:
            total = buf[0].astype(F32)
            for j in range(1, group.size):
                total = total + buf[j].astype(F32)
        to[mine, :] = total.astype(BF16)

    def back(self, stage):
        group, split = self.groups[stage]
        self.flight = []
        if not split:
            return
        sem = self.bufs[stage][0] + group.size - 1
        rows = self.part(stage, group.index)
        for step in range(1, group.size):
            copy = self.copy(sem + step - 1, self.total.at[rows, :], self.total.at[rows, :], group.member(group.after(step)))
            copy.start()
            came = self.part(stage, lax.rem(group.index + group.size - step, group.size))
            into = self.copy(sem + step - 1, self.total.at[came, :], self.total.at[came, :], group.member(group.after(step)))
            self.flight.append((copy, into))

    def arrived(self):
        for out, into in self.flight:
            out.wait_send()
            into.wait_recv()

    def steps(self):
        last = len(self.groups) - 1
        for stage in range(last + 1):
            self.go(stage)
            yield
            self.add(stage)
        for stage in range(last, -1, -1):
            if self.groups[stage][1]:
                self.back(stage)
                yield
                self.arrived()


def groups_of(where, sections, dps):
    assert sections == 4 and dps % 8 == 0
    core = where[1] % 2
    low, high = where[0] % 2, where[0] // 2
    return {
        "c": Group(where, 1, 1, 2),
        "x": Group(where, 0, 1, 2),
        "y": Group(where, 0, 2, 2),
        "p": Group(where, 0, 1, 4),
        "u": Group(where, 0, 1 + core, 2, low + core * (high - low)),
        "v": Group(where, 0, 2 - core, 2, high + core * (low - high)),
        "z": Group(where, 1, 2, 2),
        "w": Group(where, 1, 4, 2),
        "q": Group(where, 1, 2, 4),
        "r": Group(where, 1, 8, dps // 8),
    }


IN_NAMES = ("tok", "routes", "pos", "again", "abias", "qkv", "lepe", "proj", "mgain", "mbias", "fc1", "fc2", "cot")
G_NAMES = ("pos", "again", "abias", "qkv", "lepe", "proj", "mgain", "mbias", "fc1", "fc2")

LAST = 80
LANES = 128

PIECES = (
    (1536, "cpq"),
    (1536, "cpq"),
    (2048, "cpq"),
    (1536, "cpq"),
    (1536, "cpq"),
    (512, "cpq"),
    (1536, "cpq"),
    (160, "cPQ"),
)
ORDER = (
    "wait", "a1", 0, "b1", 1, "s1", 0, "c1", 1, "h1", "k1", 2, "e1", "i1", "a0", 2, 0, 3, "b0", 4, "s0",
    3, 5, "c0", 1, 4, 5, "h0", 0, "k0", 2, 6, "e0", 1, "i0", "grad", 3, 6, "l1", "p1", "l0", "p0",
    "last", "out", 0, 4, 5, 2, 7, 7, 1, 3, 6, 4, 2, 5, 0, 7, 3, 0, 6, 1, 4, 5, 1, 7, 2, 7, 6, 2, 3, 3, 4,
    5, 4, 5, 6, 6,
)


def row_map(layers):
    at, n = {}, 0
    for l in reversed(range(layers)):
        for name, rows in (("fc2", 6 * D), ("fc1", 6 * D), ("proj", 2 * D), ("qkv0", 3 * D), ("qkv1", 3 * D)):
            at[name, l] = n
            n += rows
    at["last"] = n
    return at, n + 2 * LAST


def small_map(layers):
    at, n = {}, 0
    for l in reversed(range(layers)):
        for name, rows in (("pos", 9), ("again", 1), ("abias", 1), ("lepe", 25), ("mgain", 1), ("mbias", 1)):
            at[name, l] = n
            n += rows
    assert n <= LAST
    return at


def pieces_of(layers):
    assert layers == 2
    pieces, n = [], 0
    for rows, way in PIECES:
        pieces.append((n, rows, way))
        n += rows
    assert n == row_map(layers)[1]
    return pieces


def plan(where, sections, dps, layers):
    kinds = groups_of(where, sections, dps)
    pieces = pieces_of(layers)
    plans = []
    for base, rows, way in pieces:
        if kinds["r"].size > 1:
            way += "R"
        plans.append((base, rows, [(kinds[letter.lower()], letter.islower()) for letter in way]))
    return plans


def plan_buffers(plans):
    shapes, sems = [], 0
    where = []
    for base, rows, groups in plans:
        mine = []
        for group, split in groups:
            if split:
                rows //= group.size
                shapes.append(pltpu.VMEM((group.size - 1, rows, LANES), BF16))
                mine.append((sems, len(shapes) - 1))
                sems += 2 * (group.size - 1)
            else:
                shapes.append(pltpu.VMEM((group.size, rows, LANES), BF16))
                mine.append((sems, len(shapes) - 1))
                sems += group.size - 1
        where.append(mine)
    return shapes, sems, where


def body(layers, sections, dps, names, *refs):
    k = K()
    n_in = len(IN_NAMES)
    given = dict(zip(IN_NAMES, refs[:n_in]))
    out_ref, gin_ref, total = refs[n_in : n_in + 3]
    refs = refs[n_in + 3 :]
    for name, ref in zip(names, refs):
        setattr(k, name, ref)
    refs = refs[len(names) :]
    load = refs[n_in]
    loads = {}
    for i, name in enumerate(IN_NAMES):
        setattr(k, name, refs[i])
        loads[name] = pltpu.make_async_copy(given[name], refs[i], load.at[i])
    for name in LOAD_ORDER:
        loads[name].start()
    mine, last, send, recv = refs[n_in + 1 : n_in + 5]
    bufs = refs[n_in + 5 :]

    where = (lax.axis_index("section"), lax.axis_index("dp"))
    plans = plan(where, sections, dps, layers)
    _, _, slots = plan_buffers(plans)
    barrier = pltpu.get_barrier_semaphore()
    partners = 0
    kinds = groups_of(where, sections, dps)
    for kind in "cpqr":
        group = kinds[kind]
        for step in range(1, group.size):
            pl.semaphore_signal(barrier, inc=1, device_id=group.member(group.after(step)), device_id_type=pl.DeviceIdType.MESH)
            partners += 1

    at, _ = row_map(layers)
    small_at = small_map(layers)

    def need(l, name):
        if l == 0:
            loads[name].wait()

    def store(name, l, v):
        n = at[name, l]
        v = v.astype(BF16)
        height = v.shape[0]
        for c in range(v.shape[1] // LANES):
            mine[pl.ds(n + c * height, height), :] = v[:, c * LANES : (c + 1) * LANES]

    def store_row(name, l, tap, lanes, v):
        last[pl.ds(small_at[name, l] + tap, 1), lanes] = v

    def flush(ref, n):
        for c in range(2):
            mine[pl.ds(n + c * ref.shape[0], ref.shape[0]), :] = ref[:, c * LANES : (c + 1) * LANES].astype(BF16)

    k.need = need
    k.store = store
    k.store_row = store_row
    last[...] = jnp.zeros_like(last)
    for name in LOAD_ORDER:
        if name not in LATE:
            loads[name].wait()
    prepare(k, k.tok[0, 0], k.cot[0, 0], k.routes.at[0, 0])

    for l in range(layers):
        attn_fwd(l, k)
        mlp_fwd(l, k)
    t = iota((TOKS, ROWS), 1)
    gathered = ((t >> 4) * SIDE + (t & 15) == iota((TOKS, ROWS), 0)) & valid(t)
    gathered = gathered.astype(F32).astype(BF16)

    moves = []
    for (base, rows, groups), slot in zip(plans, slots):
        moves.append(
            Exchange(mine, total, base, rows, groups, [(sem, bufs[n]) for sem, n in slot], send, recv).steps()
        )

    def finish_out():
        out_ref[0, 0] = nn(gathered, k.x[...].astype(BF16)).astype(BF16)

    def finish_grad():
        gin_ref[0, 0] = nn(gathered, k.g[...].astype(BF16)).astype(BF16)

    work = {
        "wait": lambda: pl.semaphore_wait(barrier, partners),
        "out": finish_out,
        "grad": finish_grad,
        "last": lambda: flush(last, at["last"]),
    }
    for l in range(layers):
        for name, run in (
            ("a", mlp_bwd_fc2),
            ("b", mlp_bwd),
            ("s", attn_bwd_start),
            ("l", attn_bwd_lepe),
            ("c", attn_bwd_conv),
            ("h", partial(attn_bwd_heads, half=0)),
            ("k", partial(attn_bwd_heads, half=1)),
            ("e", attn_bwd_end),
            ("i", attn_bwd_input),
            ("p", attn_bwd_pos),
        ):
            work[name + str(l)] = partial(run, l, k)
    for item in ORDER:
        if item in work:
            work[item]()
        else:
            next(moves[item], None)
    live = list(moves)
    while live:
        for m in list(live):
            if next(m, live) is live:
                live.remove(m)


def finish_body(layers, total, out_in, gin_in, *refs):
    outs = refs[:12]
    made = refs[12:24]
    sems = refs[24]
    at, _ = row_map(layers)
    small_at = small_map(layers)
    copies = []

    def go(src, dst):
        copy = pltpu.make_async_copy(src, dst, sems.at[len(copies)])
        copy.start()
        copies.append(copy)

    go(out_in, outs[0])
    go(gin_in, outs[1])
    places = dict(zip(G_NAMES, range(2, 12)))

    def wide(name, l, parts):
        ref = made[places[name]]
        for n, rows, top, col in parts:
            ref[l, pl.ds(top, rows), pl.ds(col, LANES)] = total[pl.ds(n, rows), :].astype(F32)
        go(ref.at[l], outs[places[name]].at[l])

    for l in reversed(range(layers)):
        wide("fc2", l, [(at["fc2", l] + c * 3 * D, 3 * D, 0, c * LANES) for c in range(2)])
        wide("fc1", l, [(at["fc1", l] + c * D, D, 0, c * LANES) for c in range(6)])
        wide("proj", l, [(at["proj", l] + c * D, D, 0, c * LANES) for c in range(2)])
        wide("qkv", l, [(at["qkv%d" % h, l] + c * D, D, 0, c * D + h * LANES) for c in range(3) for h in range(2)])

    def rows_from(n, count):
        return [total[pl.ds(n + c * count, count), :].astype(F32) for c in range(2)]

    both = rows_from(at["last"], LAST)
    for name, count in (("pos", 9), ("lepe", 25), ("again", 1), ("abias", 1), ("mgain", 1), ("mbias", 1)):
        ref = made[places[name]]
        for l in range(layers):
            n = small_at[name, l]
            for c in range(2):
                lanes = pl.ds(c * LANES, LANES)
                if count == 1:
                    ref[pl.ds(l, 1), lanes] = both[c][n : n + 1]
                else:
                    for tap in range(count):
                        ref[tap, pl.ds(l, 1), lanes] = both[c][n + tap : n + tap + 1]
        go(ref, outs[places[name]])
    for copy in copies:
        copy.wait()


LOAD_ORDER = ("tok", "routes", "cot", "pos", "again", "abias", "lepe", "mgain", "mbias", "qkv", "proj", "fc1", "fc2")
LATE = ("qkv", "proj", "fc1", "fc2")


def per_device(sections, dps, tokens, routes, pos, again, abias, qkv, lepe, proj, mgain, mbias, fc1, fc2, cot):
    layers = pos.shape[0]
    assert tokens.shape == (1, 1, TOKS, D)
    sc = scratch(layers)
    pos_t, lepe_t = (jnp.transpose(a, (1, 0, 2)) for a in (pos, lepe))
    routes_t = jnp.swapaxes(routes, -1, -2)
    args = (tokens, routes_t, pos_t, again, abias, qkv, lepe_t, proj, mgain, mbias, fc1, fc2, cot)
    vm = pl.BlockSpec(memory_space=pltpu.VMEM)
    hbm = pl.BlockSpec(memory_space=pl.ANY)
    _, count = row_map(layers)
    shapes, sems, _ = plan_buffers(plan((0, 0), sections, dps, layers))
    params = pltpu.CompilerParams(vmem_limit_bytes=58 * 2**20, collective_id=0, has_side_effects=True)
    out, gin, total = pl.pallas_call(
        partial(body, layers, sections, dps, tuple(sc)),
        out_shape=[pltpu.VMEM(tokens.shape, BF16)] * 2 + [pltpu.VMEM((count, LANES), BF16)],
        in_specs=[hbm] * len(args),
        out_specs=[vm] * 3,
        scratch_shapes=list(sc.values())
        + [pltpu.VMEM(a.shape, a.dtype) for a in args]
        + [
            pltpu.SemaphoreType.DMA((len(args),)),
            pltpu.VMEM((count, LANES), BF16),
            pltpu.VMEM((LAST, D), F32),
            pltpu.SemaphoreType.DMA((sems,)),
            pltpu.SemaphoreType.DMA((sems,)),
        ]
        + shapes,
        compiler_params=params,
        name="blocks",
    )(*args)
    weights = (pos_t, again, abias, qkv, lepe_t, proj, mgain, mbias, fc1, fc2)
    shapes = [jax.ShapeDtypeStruct(tokens.shape, BF16)] * 2 + [jax.ShapeDtypeStruct(w.shape, F32) for w in weights]
    res = pl.pallas_call(
        partial(finish_body, layers),
        out_shape=shapes,
        in_specs=[vm] * 3,
        out_specs=[hbm] * 12,
        scratch_shapes=[pltpu.VMEM(a.shape, a.dtype) for a in shapes] + [pltpu.SemaphoreType.DMA((2 + 4 * layers + 6,))],
        compiler_params=pltpu.CompilerParams(vmem_limit_bytes=32 * 2**20),
        name="widen",
    )(total, out, gin)
    res = list(res)
    res[2] = jnp.transpose(res[2], (1, 0, 2))
    res[6] = jnp.transpose(res[6], (1, 0, 2))
    return tuple(res)


def solution(mesh):
    image = P("section", "dp", None, None)
    sections, dps = mesh.shape["section"], mesh.shape["dp"]
    return jax.shard_map(
        partial(per_device, sections, dps),
        mesh=mesh,
        in_specs=(image, P("section", "dp", None, None, None, None)) + (P(),) * 10 + (image,),
        out_specs=(image, image) + (P(),) * 10,
        check_vma=False,
    )
```

```python
from functools import partial
import math

import jax
import jax.numpy as jnp
from jax import lax
from jax.experimental import pallas as pl
from jax.experimental.pallas import tpu as pltpu
from jax.sharding import PartitionSpec as P

F32 = jnp.float32
BF16 = jnp.bfloat16
EPS = 1e-06
HEADS = 8
SIDE = 14
WIDE = 16
TOKS = SIDE * SIDE
ROWS = SIDE * WIDE
FULL = 256
D = 256
HD = 32
REGIONS = 49
TOPK = 4
BLOCKED = -1e30
LOG2E = 1.4426950408889634


def nn(a, b):
    return lax.dot_general(a, b, (((1,), (0,)), ((), ())), preferred_element_type=F32)


def nt(a, b):
    return lax.dot_general(a, b, (((1,), (1,)), ((), ())), preferred_element_type=F32)


def tn(a, b):
    return lax.dot_general(a, b, (((0,), (0,)), ((), ())), preferred_element_type=F32)


def iota(shape, dim):
    return lax.broadcasted_iota(jnp.int32, shape, dim)


def region_of(t):
    return (t >> 5) * (SIDE // 2) + ((t & 15) >> 1)


def valid(t):
    return ((t & 15) < SIDE) & (t < ROWS)


def keep_rows():
    return valid(iota((ROWS, 1), 0))


def norm_parts(v):
    mean = jnp.sum(v, axis=-1, keepdims=True) * (1.0 / D)
    cen = v - mean
    var = jnp.sum(cen * cen, axis=-1, keepdims=True) * (1.0 / D)
    rstd = lax.rsqrt(var + EPS)
    return cen * rstd, rstd


def shifted_into(s_ref, x, extent):
    radius = extent // 2
    for b in range(extent):
        away = b - radius
        s_ref[b, pl.ds(32, ROWS), :] = x if away == 0 else pltpu.roll(x, (-away) % ROWS, 0)


CH = 112


def conv_from(s_ref, taps, extent, flip, base, out_ref):
    radius = extent // 2
    for half in range(2):
        lanes = pl.ds(half * 128, 128)
        for c in range(ROWS // CH):
            acc = None
            for a in range(extent):
                for b in range(extent):
                    tap = a * extent + b
                    if flip:
                        tap = extent * extent - 1 - tap
                    part = s_ref[b, pl.ds(32 + c * CH + 16 * (a - radius), CH), lanes]
                    part = part * taps[pl.ds(tap, 1), lanes]
                    acc = part if acc is None else acc + part
            rows = pl.ds(c * CH, CH)
            if base is not None:
                acc = acc + base[rows, lanes]
            out_ref[rows, lanes] = acc


def conv_taps_grad(s_ref, d_ref, extent, store):
    radius = extent // 2
    for half in range(2):
        lanes = pl.ds(half * 128, 128)
        sums = [None] * (extent * extent)
        for c in range(ROWS // CH):
            d = d_ref[pl.ds(c * CH, CH), lanes]
            for a in range(extent):
                for b in range(extent):
                    part = s_ref[b, pl.ds(32 + c * CH + 16 * (a - radius), CH), lanes] * d
                    part = jnp.sum(part.reshape(CH // 8, 8, 128), axis=0)
                    tap = a * extent + b
                    sums[tap] = part if sums[tap] is None else sums[tap] + part
        for tap, s in enumerate(sums):
            store(tap, lanes, jnp.sum(s, axis=0, keepdims=True))


def head_keys(half):
    lane = iota((1, 128), 1)
    parts = []
    for hh in range(4):
        own = (lane >= hh * HD) & (lane < (hh + 1) * HD)
        parts.append(jnp.where(own, half, jnp.zeros_like(half)))
    return jnp.concatenate(parts, 0)


def gelu_pair(x):
    cdf = 0.5 * (1.0 + lax.erf(x * (2.0**-0.5)))
    pdf = jnp.exp2(x * x * (-0.5 * LOG2E)) * (1.0 / math.sqrt(2.0 * math.pi))
    return x * cdf, cdf + x * pdf


class K:
    pass


def attn_fwd(l, k):
    x = k.x[...]
    shifted_into(k.sx.at[l], x, 3)
    conv_from(k.sx.at[l], k.posf.at[l], 3, False, k.x, k.tmp)
    mixed = k.tmp[...]
    xhat, rstd = norm_parts(mixed)
    k.a_xhat[l] = xhat
    k.a_rstd[l] = rstd
    gain = k.againf[pl.ds(l, 1), :]
    bias = k.abiasf[pl.ds(l, 1), :]
    normed = jnp.where(keep_rows(), xhat * gain + bias, 0.0).astype(BF16)
    k.a_normed[l] = normed
    k.need(l, "qkv")
    packed = nn(normed, k.qkv[l]).astype(BF16)
    q = packed[:, :D]
    key = packed[:, D : 2 * D]
    val = packed[:, 2 * D :]
    k.key[l] = key
    k.val[l] = val
    zpad = jnp.zeros((FULL - ROWS, D), BF16)
    qT, kT, vT = (jnp.concatenate([part, zpad], 0).T for part in (q, key, val))
    k.qT[l] = qT
    k.kT[l] = kT
    shifted_into(k.sv.at[l], val.astype(F32), 5)
    conv_from(k.sv.at[l], k.lepef.at[l], 5, False, None, k.tmp2)
    eqT = k.eqT[...]
    c = HD**-0.5 * LOG2E
    zkeys = jnp.zeros((FULL - ROWS, FULL), BF16)
    outs = []
    for half in range(2):
        lanes = slice(half * 128, half * 128 + 128)
        heads = pl.ds(l * HEADS + half * 4, 4)
        rhs = jnp.concatenate([qT[lanes], eqT], 0)
        lhs = jnp.concatenate([head_keys(key[:, lanes]), k.blocked[heads].reshape(4 * ROWS, 128)], 1)
        s = nn(lhs, rhs).reshape(4, ROWS, FULL)
        m = jnp.max(s, axis=1, keepdims=True)
        e = jnp.exp2((s - m) * c)
        p = e * (1.0 / jnp.sum(e, axis=1, keepdims=True))
        k.p[heads] = p
        pb = p.astype(BF16)
        k.pb[heads, :ROWS] = pb
        for hh in range(4):
            h = half * 4 + hh
            outs.append(nn(vT[h * HD : (h + 1) * HD], jnp.concatenate([pb[hh], zkeys], 0)))
    ctx = (jnp.concatenate(outs, 0).T[:ROWS] + k.tmp2[...]).astype(BF16)
    k.ctx[l] = ctx
    k.need(l, "proj")
    res = k.tmp[...] + nn(ctx, k.proj[l])
    k.x[...] = jnp.where(keep_rows(), res, 0.0).astype(BF16).astype(F32)


def mlp_fwd(l, k):
    x = k.x[...]
    xhat, rstd = norm_parts(x)
    k.m_xhat[l] = xhat
    k.m_rstd[l] = rstd
    normed = (xhat * k.mgainf[pl.ds(l, 1), :] + k.mbiasf[pl.ds(l, 1), :]).astype(BF16)
    k.m_normed[l] = normed
    k.need(l, "fc1")
    hidden = nn(normed, k.fc1[l])
    act, slope = gelu_pair(hidden)
    act = act.astype(BF16)
    k.act[l] = act
    k.slope[l] = slope
    k.need(l, "fc2")
    res = x + nn(act, k.fc2[l])
    k.x[...] = jnp.where(keep_rows(), res, 0.0).astype(BF16).astype(F32)


def norm_bwd(dy, xhat, rstd, gain, store_gain, store_bias):
    store_gain(jnp.sum(dy * xhat, axis=0, keepdims=True))
    store_bias(jnp.sum(dy, axis=0, keepdims=True))
    dg = dy * gain
    m1 = jnp.sum(dg, axis=-1, keepdims=True) * (1.0 / D)
    m2 = jnp.sum(dg * xhat, axis=-1, keepdims=True) * (1.0 / D)
    return rstd * (dg - m1 - xhat * m2)


def mlp_bwd_fc2(l, k):
    k.store("fc2", l, tn(k.act[l], k.g[...].astype(BF16)))


def mlp_bwd(l, k):
    g = k.g[...]
    gb = g.astype(BF16)
    dact = nt(gb, k.fc2[l]).astype(BF16).astype(F32)
    dhid = (k.slope[l] * dact).astype(BF16)
    k.store("fc1", l, tn(k.m_normed[l], dhid))
    dn = nt(dhid, k.fc1[l]).astype(BF16).astype(F32)
    dx = norm_bwd(
        dn,
        k.m_xhat[l],
        k.m_rstd[l],
        k.mgainf[pl.ds(l, 1), :],
        lambda v: k.store_row("mgain", l, 0, slice(None), v),
        lambda v: k.store_row("mbias", l, 0, slice(None), v),
    )
    k.g[...] = (dx + g).astype(BF16).astype(F32)


def attn_bwd_start(l, k):
    g = k.g[...]
    gb = g.astype(BF16)
    k.store("proj", l, tn(k.ctx[l], gb))
    dctx = nt(gb, k.proj[l]).astype(BF16)
    dctx32 = dctx.astype(F32)
    k.dctx[l] = dctx32
    zpad = jnp.zeros((FULL - ROWS, D), BF16)
    k.dcT[...] = jnp.concatenate([dctx, zpad], 0).T
    shifted_into(k.sd, dctx32, 5)


def attn_bwd_lepe(l, k):
    conv_taps_grad(k.sv.at[l], k.dctx.at[l], 5, lambda tap, lanes, v: k.store_row("lepe", l, tap, lanes, v))


def attn_bwd_conv(l, k):
    conv_from(k.sd, k.lepef.at[l], 5, True, None, k.tmp2)


def attn_bwd_heads(l, k, half):
    scale = HD**-0.5
    lanes = slice(half * 128, half * 128 + 128)
    heads = pl.ds(l * HEADS + half * 4, 4)
    dcT = k.dcT[lanes]
    qT, kT = k.qT[l, lanes], k.kT[l, lanes]
    dp = nn(head_keys(k.val[l, :, lanes]), dcT).reshape(4, ROWS, FULL)
    p = k.p[heads]
    pb = k.pb[heads]
    pd = p * dp
    ds = (pd - p * jnp.sum(pd, axis=1, keepdims=True)).astype(BF16)
    zkeys = jnp.zeros((FULL - ROWS, FULL), BF16)
    dq, dk, dv = [], [], []
    for hh in range(4):
        rows = slice(hh * HD, (hh + 1) * HD)
        dsb = jnp.concatenate([ds[hh], zkeys], 0)
        dv.append(nt(dcT[rows], pb[hh]))
        dq.append(nn(kT[rows], dsb))
        dk.append(nt(qT[rows], dsb))
    dq, dk, dv = (jnp.concatenate(part, 0).T[:ROWS] for part in (dq, dk, dv))
    dq = (dq * scale).astype(BF16)
    dk = (dk * scale).astype(BF16)
    dv = jnp.where(keep_rows(), dv + k.tmp2[:, lanes], 0.0).astype(BF16)
    k.dpacked[:, lanes] = dq
    k.dpacked[:, slice(D + half * 128, D + half * 128 + 128)] = dk
    k.dpacked[:, slice(2 * D + half * 128, 2 * D + half * 128 + 128)] = dv
    k.store("qkv%d" % half, l, tn(k.a_normed[l], jnp.concatenate([dq, dk, dv], 1)))


def attn_bwd_end(l, k):
    g = k.g[...]
    dn = nt(k.dpacked[...], k.qkv[l]).astype(BF16).astype(F32)
    dx = norm_bwd(
        dn,
        k.a_xhat[l],
        k.a_rstd[l],
        k.againf[pl.ds(l, 1), :],
        lambda v: k.store_row("again", l, 0, slice(None), v),
        lambda v: k.store_row("abias", l, 0, slice(None), v),
    )
    dmixed = dx + g
    k.dmixed[l] = dmixed


def attn_bwd_pos(l, k):
    conv_taps_grad(k.sx.at[l], k.dmixed.at[l], 3, lambda tap, lanes, v: k.store_row("pos", l, tap, lanes, v))


def attn_bwd_input(l, k):
    shifted_into(k.sd, k.dmixed[l], 3)
    conv_from(k.sd, k.posf.at[l], 3, True, k.dmixed.at[l], k.tmp2)
    k.g[...] = jnp.where(keep_rows(), k.tmp2[...], 0.0).astype(BF16).astype(F32)


def prepare(k, tok, cot, routes):
    t = iota((ROWS, TOKS), 0)
    spread = ((t >> 4) * SIDE + (t & 15) == iota((ROWS, TOKS), 1)) & valid(t)
    spread = spread.astype(F32).astype(BF16)
    k.x[...] = nn(spread, tok)
    k.g[...] = nn(spread, cot)
    t = iota((ROWS, 128), 0)
    reg = jnp.where(valid(t), region_of(t), REGIONS)
    k.ekey[...] = (reg == iota((ROWS, 128), 1)).astype(F32).astype(BF16)
    t = iota((128, FULL), 1)
    k.eqT[...] = ((region_of(t) == iota((128, FULL), 0)) & valid(t)).astype(F32).astype(BF16)
    place = iota((128, REGIONS), 0)
    k.open[...] = jnp.zeros_like(k.open)
    k.pb[:, ROWS:, :] = jnp.zeros((k.pb.shape[0], FULL - ROWS, FULL), BF16)
    for ref in (k.sx, k.sv):
        for l in range(ref.shape[0]):
            for b in range(ref.shape[1]):
                ref[l, b, :32] = jnp.zeros((32, D), F32)
                ref[l, b, 32 + ROWS :] = jnp.zeros((32, D), F32)
    for b in range(5):
        k.sd[b, :32] = jnp.zeros((32, D), F32)
        k.sd[b, 32 + ROWS :] = jnp.zeros((32, D), F32)
    ekey = k.ekey[...]
    for lh in range(k.blocked.shape[0]):
        hit = None
        for j in range(TOPK):
            same = routes[lh // HEADS, lh % HEADS, pl.ds(j, 1), :] == place
            hit = same if hit is None else hit | same
        k.open[lh, :, :REGIONS] = jnp.where(hit, 0.0, BLOCKED).astype(BF16)
    for lh in range(0, k.blocked.shape[0], 2):
        both = nn(ekey, jnp.concatenate([k.open[lh], k.open[lh + 1]], 1)).astype(BF16)
        k.blocked[lh] = both[:, :128]
        k.blocked[lh + 1] = both[:, 128:]
    k.againf[:k.again.shape[0], :] = k.again[...].astype(F32)
    k.abiasf[:k.abias.shape[0], :] = k.abias[...].astype(F32)
    k.mgainf[:k.mgain.shape[0], :] = k.mgain[...].astype(F32)
    k.mbiasf[:k.mbias.shape[0], :] = k.mbias[...].astype(F32)
    for tap in range(9):
        k.posf[:, tap, :] = k.pos[tap].astype(F32)
    for tap in range(25):
        k.lepef[:, tap, :] = k.lepe[tap].astype(F32)


def scratch(layers):
    one = pltpu.VMEM
    return dict(
        againf=one((8, D), F32),
        abiasf=one((8, D), F32),
        mgainf=one((8, D), F32),
        mbiasf=one((8, D), F32),
        posf=one((layers, 16, D), F32),
        lepef=one((layers, 32, D), F32),
        x=one((ROWS, D), F32),
        g=one((ROWS, D), F32),
        tmp=one((ROWS, D), F32),
        tmp2=one((ROWS, D), F32),
        sx=one((layers, 3, 64 + ROWS, D), F32),
        sv=one((layers, 5, 64 + ROWS, D), F32),
        sd=one((5, 64 + ROWS, D), F32),
        a_xhat=one((layers, ROWS, D), F32),
        a_rstd=one((layers, ROWS, 1), F32),
        a_normed=one((layers, ROWS, D), BF16),
        key=one((layers, ROWS, D), BF16),
        val=one((layers, ROWS, D), BF16),
        qT=one((layers, D, FULL), BF16),
        kT=one((layers, D, FULL), BF16),
        dcT=one((D, FULL), BF16),
        dpacked=one((ROWS, 3 * D), BF16),
        dctx=one((layers, ROWS, D), F32),
        dmixed=one((layers, ROWS, D), F32),
        p=one((layers * HEADS, ROWS, FULL), F32),
        pb=one((layers * HEADS, FULL, FULL), BF16),
        blocked=one((layers * HEADS, ROWS, 128), BF16),
        open=one((layers * HEADS, 128, 128), BF16),
        ekey=one((ROWS, 128), BF16),
        eqT=one((128, FULL), BF16),
        ctx=one((layers, ROWS, D), BF16),
        m_xhat=one((layers, ROWS, D), F32),
        m_rstd=one((layers, ROWS, 1), F32),
        m_normed=one((layers, ROWS, D), BF16),
        act=one((layers, ROWS, 3 * D), BF16),
        slope=one((layers, ROWS, 3 * D), F32),
    )


class Group:
    def __init__(self, where, axis, stride, size, index=None):
        self.where, self.axis, self.stride, self.size = where, axis, stride, size
        self.index = (where[axis] // stride) % size if index is None else index

    def member(self, j):
        at = list(self.where)
        at[self.axis] = self.where[self.axis] + (j - self.index) * self.stride
        return tuple(at)

    def after(self, step):
        return lax.rem(self.index + step, self.size)


class Exchange:
    def __init__(self, mine, total, base, rows, groups, bufs, send, recv):
        self.mine, self.total, self.groups = mine, total, groups
        self.bufs, self.send, self.recv = bufs, send, recv
        self.base, self.rows = [base], [rows]
        for group, split in groups:
            size = self.rows[-1] // group.size if split else self.rows[-1]
            self.rows.append(size)
            self.base.append(self.base[-1] + group.index * size if split else self.base[-1])
        self.flight, self.owed = None, []

    def part(self, stage, j):
        size = self.rows[stage + 1]
        return pl.ds(pl.multiple_of(self.base[stage] + j * size, 16), size)

    def own(self, stage):
        return pl.ds(pl.multiple_of(self.base[stage], 16), self.rows[stage])

    def copy(self, sem, src, dst, to):
        return pltpu.make_async_remote_copy(
            src_ref=src,
            dst_ref=dst,
            send_sem=self.send.at[sem],
            recv_sem=self.recv.at[sem],
            device_id=to,
            device_id_type=pl.DeviceIdType.MESH,
        )

    def started(self, sem, like):
        self.flight = self.copy(sem, like, like, self.groups[0][0].member(self.groups[0][0].after(1)))
        self.owed.append(self.flight)

    def go(self, stage):
        group, split = self.groups[stage]
        sem, buf = self.bufs[stage]
        others = group.size - 1
        if not split:
            buf[group.index] = self.mine[self.own(stage), :]
        for step in range(1, group.size):
            to = group.after(step)
            if split:
                src, dst = self.mine.at[self.part(stage, to), :], buf.at[step - 1]
            else:
                src, dst = self.mine.at[self.own(stage), :], buf.at[group.index]
            self.copy(sem, src, dst, group.member(to)).start()
        self.started(sem, buf if split else buf.at[pl.ds(0, others)])

    def add(self, stage):
        group, split = self.groups[stage]
        _, buf = self.bufs[stage]
        if not split:
            self.owed.pop().wait_send()
        self.flight.wait_recv()
        mine = self.own(stage + 1)
        last = stage + 1 == len(self.groups)
        to = self.total if last else self.mine
        if split:
            total = self.mine[mine, :].astype(F32)
            for step in range(group.size - 1):
                total = total + buf[step].astype(F32)
        else:
            total = buf[0].astype(F32)
            for j in range(1, group.size):
                total = total + buf[j].astype(F32)
        to[mine, :] = total.astype(BF16)

    def back(self, stage):
        group, _ = self.groups[stage]
        sem = self.bufs[stage][0] + 1
        rows = self.part(stage, group.index)
        for step in range(1, group.size):
            self.copy(sem, self.total.at[rows, :], self.total.at[rows, :], group.member(group.after(step))).start()
        others = (group.size - 1) * self.rows[stage + 1]
        self.started(sem, self.total.at[pl.ds(pl.multiple_of(self.base[stage], 16), others), :])

    def steps(self):
        last = len(self.groups) - 1
        for stage in range(last + 1):
            self.go(stage)
            yield
            self.add(stage)
        ways = [stage for stage in range(last, -1, -1) if self.groups[stage][1]]
        for stage in ways:
            self.back(stage)
            yield
            if stage == ways[-1]:
                for sent in self.owed:
                    sent.wait_send()
            self.flight.wait_recv()


def groups_of(where, sections, dps):
    assert sections == 4 and dps % 8 == 0
    core = where[1] % 2
    low, high = where[0] % 2, where[0] // 2
    return {
        "c": Group(where, 1, 1, 2),
        "x": Group(where, 0, 1, 2),
        "y": Group(where, 0, 2, 2),
        "p": Group(where, 0, 1, 4),
        "u": Group(where, 0, 1 + core, 2, low + core * (high - low)),
        "v": Group(where, 0, 2 - core, 2, high + core * (low - high)),
        "z": Group(where, 1, 2, 2),
        "w": Group(where, 1, 4, 2),
        "q": Group(where, 1, 2, 4),
        "r": Group(where, 1, 8, dps // 8),
    }


IN_NAMES = ("tok", "routes", "pos", "again", "abias", "qkv", "lepe", "proj", "mgain", "mbias", "fc1", "fc2", "cot")
G_NAMES = ("pos", "again", "abias", "qkv", "lepe", "proj", "mgain", "mbias", "fc1", "fc2")

LAST = 80
LANES = 128

PIECES = (
    (1536, "cpq"),
    (1536, "cpq"),
    (2048, "cpq"),
    (1536, "cpq"),
    (1536, "cpq"),
    (512, "cpq"),
    (1536, "cpq"),
    (160, "cPQ"),
)
ORDER = (
    "wait", "a1", 0, "b1", 1, "s1", 0, "c1", 1, "h1", "k1", 2, "e1", "i1", "a0", 2, 0, 3, "b0", 4, "s0",
    3, 5, "c0", 1, 4, 5, "h0", 0, "k0", 2, 6, "e0", 1, "i0", "grad", 3, 6, "l1", "p1", "l0", "p0",
    "last", "out", 0, 4, 5, 2, 7, 7, 1, 3, 6, 4, 2, 5, 0, 7, 3, 0, 6, 1, 4, 5, 1, 7, 2, 7, 6, 2, 3, 3, 4,
    5, 4, 5, 6, 6,
)


def row_map(layers):
    at, n = {}, 0
    for l in reversed(range(layers)):
        for name, rows in (("fc2", 6 * D), ("fc1", 6 * D), ("proj", 2 * D), ("qkv0", 3 * D), ("qkv1", 3 * D)):
            at[name, l] = n
            n += rows
    at["last"] = n
    return at, n + 2 * LAST


def small_map(layers):
    at, n = {}, 0
    for l in reversed(range(layers)):
        for name, rows in (("pos", 9), ("again", 1), ("abias", 1), ("lepe", 25), ("mgain", 1), ("mbias", 1)):
            at[name, l] = n
            n += rows
    assert n <= LAST
    return at


def pieces_of(layers):
    assert layers == 2
    pieces, n = [], 0
    for rows, way in PIECES:
        pieces.append((n, rows, way))
        n += rows
    assert n == row_map(layers)[1]
    return pieces


def plan(where, sections, dps, layers):
    kinds = groups_of(where, sections, dps)
    pieces = pieces_of(layers)
    plans = []
    for base, rows, way in pieces:
        if kinds["r"].size > 1:
            way += "R"
        plans.append((base, rows, [(kinds[letter.lower()], letter.islower()) for letter in way]))
    return plans


def plan_buffers(plans):
    shapes, sems = [], 0
    where = []
    for base, rows, groups in plans:
        mine = []
        for group, split in groups:
            if split:
                rows //= group.size
                shapes.append(pltpu.VMEM((group.size - 1, rows, LANES), BF16))
                mine.append((sems, len(shapes) - 1))
                sems += 2
            else:
                shapes.append(pltpu.VMEM((group.size, rows, LANES), BF16))
                mine.append((sems, len(shapes) - 1))
                sems += 1
        where.append(mine)
    return shapes, sems, where


def body(layers, sections, dps, names, *refs):
    k = K()
    n_in = len(IN_NAMES)
    given = dict(zip(IN_NAMES, refs[:n_in]))
    out_ref, gin_ref, total = refs[n_in : n_in + 3]
    refs = refs[n_in + 3 :]
    for name, ref in zip(names, refs):
        setattr(k, name, ref)
    refs = refs[len(names) :]
    load = refs[n_in]
    loads = {}
    for i, name in enumerate(IN_NAMES):
        setattr(k, name, refs[i])
        loads[name] = pltpu.make_async_copy(given[name], refs[i], load.at[i])
    for name in LOAD_ORDER:
        loads[name].start()
    mine, last, send, recv = refs[n_in + 1 : n_in + 5]
    bufs = refs[n_in + 5 :]

    where = (lax.axis_index("section"), lax.axis_index("dp"))
    plans = plan(where, sections, dps, layers)
    _, _, slots = plan_buffers(plans)
    barrier = pltpu.get_barrier_semaphore()
    partners = 0
    kinds = groups_of(where, sections, dps)
    for kind in "cpqr":
        group = kinds[kind]
        for step in range(1, group.size):
            pl.semaphore_signal(barrier, inc=1, device_id=group.member(group.after(step)), device_id_type=pl.DeviceIdType.MESH)
            partners += 1

    at, _ = row_map(layers)
    small_at = small_map(layers)

    def need(l, name):
        if l == 0:
            loads[name].wait()

    def store(name, l, v):
        n = at[name, l]
        v = v.astype(BF16)
        height = v.shape[0]
        for c in range(v.shape[1] // LANES):
            mine[pl.ds(n + c * height, height), :] = v[:, c * LANES : (c + 1) * LANES]

    def store_row(name, l, tap, lanes, v):
        last[pl.ds(small_at[name, l] + tap, 1), lanes] = v

    def flush(ref, n):
        for c in range(2):
            mine[pl.ds(n + c * ref.shape[0], ref.shape[0]), :] = ref[:, c * LANES : (c + 1) * LANES].astype(BF16)

    k.need = need
    k.store = store
    k.store_row = store_row
    last[...] = jnp.zeros_like(last)
    for name in LOAD_ORDER:
        if name not in LATE:
            loads[name].wait()
    prepare(k, k.tok[0, 0], k.cot[0, 0], k.routes.at[0, 0])

    for l in range(layers):
        attn_fwd(l, k)
        mlp_fwd(l, k)
    t = iota((TOKS, ROWS), 1)
    gathered = ((t >> 4) * SIDE + (t & 15) == iota((TOKS, ROWS), 0)) & valid(t)
    gathered = gathered.astype(F32).astype(BF16)

    moves = []
    for (base, rows, groups), slot in zip(plans, slots):
        moves.append(
            Exchange(mine, total, base, rows, groups, [(sem, bufs[n]) for sem, n in slot], send, recv).steps()
        )

    def finish_out():
        out_ref[0, 0] = nn(gathered, k.x[...].astype(BF16)).astype(BF16)

    def finish_grad():
        gin_ref[0, 0] = nn(gathered, k.g[...].astype(BF16)).astype(BF16)

    work = {
        "wait": lambda: pl.semaphore_wait(barrier, partners),
        "out": finish_out,
        "grad": finish_grad,
        "last": lambda: flush(last, at["last"]),
    }
    for l in range(layers):
        for name, run in (
            ("a", mlp_bwd_fc2),
            ("b", mlp_bwd),
            ("s", attn_bwd_start),
            ("l", attn_bwd_lepe),
            ("c", attn_bwd_conv),
            ("h", partial(attn_bwd_heads, half=0)),
            ("k", partial(attn_bwd_heads, half=1)),
            ("e", attn_bwd_end),
            ("i", attn_bwd_input),
            ("p", attn_bwd_pos),
        ):
            work[name + str(l)] = partial(run, l, k)
    for item in ORDER:
        if item in work:
            work[item]()
        else:
            next(moves[item], None)
    live = list(moves)
    while live:
        for m in list(live):
            if next(m, live) is live:
                live.remove(m)


def finish_body(layers, total, out_in, gin_in, *refs):
    outs = refs[:12]
    made = refs[12:24]
    sems = refs[24]
    at, _ = row_map(layers)
    small_at = small_map(layers)
    copies = []

    def go(src, dst):
        copy = pltpu.make_async_copy(src, dst, sems.at[len(copies)])
        copy.start()
        copies.append(copy)

    go(out_in, outs[0])
    go(gin_in, outs[1])
    places = dict(zip(G_NAMES, range(2, 12)))

    def wide(name, l, parts):
        ref = made[places[name]]
        for n, rows, top, col in parts:
            ref[l, pl.ds(top, rows), pl.ds(col, LANES)] = total[pl.ds(n, rows), :].astype(F32)
        go(ref.at[l], outs[places[name]].at[l])

    for l in reversed(range(layers)):
        wide("fc2", l, [(at["fc2", l] + c * 3 * D, 3 * D, 0, c * LANES) for c in range(2)])
        wide("fc1", l, [(at["fc1", l] + c * D, D, 0, c * LANES) for c in range(6)])
        wide("proj", l, [(at["proj", l] + c * D, D, 0, c * LANES) for c in range(2)])
        wide("qkv", l, [(at["qkv%d" % h, l] + c * D, D, 0, c * D + h * LANES) for c in range(3) for h in range(2)])

    def rows_from(n, count):
        return [total[pl.ds(n + c * count, count), :].astype(F32) for c in range(2)]

    both = rows_from(at["last"], LAST)
    for name, count in (("pos", 9), ("lepe", 25), ("again", 1), ("abias", 1), ("mgain", 1), ("mbias", 1)):
        ref = made[places[name]]
        for l in range(layers):
            n = small_at[name, l]
            for c in range(2):
                lanes = pl.ds(c * LANES, LANES)
                if count == 1:
                    ref[pl.ds(l, 1), lanes] = both[c][n : n + 1]
                else:
                    for tap in range(count):
                        ref[tap, pl.ds(l, 1), lanes] = both[c][n + tap : n + tap + 1]
        go(ref, outs[places[name]])
    for copy in copies:
        copy.wait()


LOAD_ORDER = ("tok", "routes", "cot", "pos", "again", "abias", "lepe", "mgain", "mbias", "qkv", "proj", "fc1", "fc2")
LATE = ("qkv", "proj", "fc1", "fc2")


def per_device(sections, dps, tokens, routes, pos, again, abias, qkv, lepe, proj, mgain, mbias, fc1, fc2, cot):
    layers = pos.shape[0]
    assert tokens.shape == (1, 1, TOKS, D)
    sc = scratch(layers)
    pos_t, lepe_t = (jnp.transpose(a, (1, 0, 2)) for a in (pos, lepe))
    routes_t = jnp.swapaxes(routes, -1, -2)
    args = (tokens, routes_t, pos_t, again, abias, qkv, lepe_t, proj, mgain, mbias, fc1, fc2, cot)
    vm = pl.BlockSpec(memory_space=pltpu.VMEM)
    hbm = pl.BlockSpec(memory_space=pl.ANY)
    _, count = row_map(layers)
    shapes, sems, _ = plan_buffers(plan((0, 0), sections, dps, layers))
    params = pltpu.CompilerParams(vmem_limit_bytes=58 * 2**20, collective_id=0, has_side_effects=True)
    out, gin, total = pl.pallas_call(
        partial(body, layers, sections, dps, tuple(sc)),
        out_shape=[pltpu.VMEM(tokens.shape, BF16)] * 2 + [pltpu.VMEM((count, LANES), BF16)],
        in_specs=[hbm] * len(args),
        out_specs=[vm] * 3,
        scratch_shapes=list(sc.values())
        + [pltpu.VMEM(a.shape, a.dtype) for a in args]
        + [
            pltpu.SemaphoreType.DMA((len(args),)),
            pltpu.VMEM((count, LANES), BF16),
            pltpu.VMEM((LAST, D), F32),
            pltpu.SemaphoreType.DMA((sems,)),
            pltpu.SemaphoreType.DMA((sems,)),
        ]
        + shapes,
        compiler_params=params,
        name="blocks",
    )(*args)
    weights = (pos_t, again, abias, qkv, lepe_t, proj, mgain, mbias, fc1, fc2)
    shapes = [jax.ShapeDtypeStruct(tokens.shape, BF16)] * 2 + [jax.ShapeDtypeStruct(w.shape, F32) for w in weights]
    res = pl.pallas_call(
        partial(finish_body, layers),
        out_shape=shapes,
        in_specs=[vm] * 3,
        out_specs=[hbm] * 12,
        scratch_shapes=[pltpu.VMEM(a.shape, a.dtype) for a in shapes] + [pltpu.SemaphoreType.DMA((2 + 4 * layers + 6,))],
        compiler_params=pltpu.CompilerParams(vmem_limit_bytes=32 * 2**20),
        name="widen",
    )(total, out, gin)
    res = list(res)
    res[2] = jnp.transpose(res[2], (1, 0, 2))
    res[6] = jnp.transpose(res[6], (1, 0, 2))
    return tuple(res)


def solution(mesh):
    image = P("section", "dp", None, None)
    sections, dps = mesh.shape["section"], mesh.shape["dp"]
    return jax.shard_map(
        partial(per_device, sections, dps),
        mesh=mesh,
        in_specs=(image, P("section", "dp", None, None, None, None)) + (P(),) * 10 + (image,),
        out_specs=(image, image) + (P(),) * 10,
        check_vma=False,
    )
```

```python
from functools import partial
import math

import jax
import jax.numpy as jnp
from jax import lax
from jax.experimental import pallas as pl
from jax.experimental.pallas import tpu as pltpu
from jax.sharding import PartitionSpec as P

F32 = jnp.float32
BF16 = jnp.bfloat16
EPS = 1e-06
HEADS = 8
SIDE = 14
WIDE = 16
TOKS = SIDE * SIDE
ROWS = SIDE * WIDE
FULL = 256
D = 256
HD = 32
REGIONS = 49
TOPK = 4
BLOCKED = -1e30
LOG2E = 1.4426950408889634


def nn(a, b):
    return lax.dot_general(a, b, (((1,), (0,)), ((), ())), preferred_element_type=F32)


def nt(a, b):
    return lax.dot_general(a, b, (((1,), (1,)), ((), ())), preferred_element_type=F32)


def tn(a, b):
    return lax.dot_general(a, b, (((0,), (0,)), ((), ())), preferred_element_type=F32)


def iota(shape, dim):
    return lax.broadcasted_iota(jnp.int32, shape, dim)


def region_of(t):
    return (t >> 5) * (SIDE // 2) + ((t & 15) >> 1)


def valid(t):
    return ((t & 15) < SIDE) & (t < ROWS)


def keep_rows():
    return valid(iota((ROWS, 1), 0))


def norm_parts(v):
    mean = jnp.sum(v, axis=-1, keepdims=True) * (1.0 / D)
    cen = v - mean
    var = jnp.sum(cen * cen, axis=-1, keepdims=True) * (1.0 / D)
    rstd = lax.rsqrt(var + EPS)
    return cen * rstd, rstd


def shifted_into(s_ref, x, extent):
    radius = extent // 2
    for b in range(extent):
        away = b - radius
        s_ref[b, pl.ds(32, ROWS), :] = x if away == 0 else pltpu.roll(x, (-away) % ROWS, 0)


CH = 112


def conv_from(s_ref, taps, extent, flip, base, out_ref):
    radius = extent // 2
    for half in range(2):
        lanes = pl.ds(half * 128, 128)
        for c in range(ROWS // CH):
            acc = None
            for a in range(extent):
                for b in range(extent):
                    tap = a * extent + b
                    if flip:
                        tap = extent * extent - 1 - tap
                    part = s_ref[b, pl.ds(32 + c * CH + 16 * (a - radius), CH), lanes]
                    part = part * taps[pl.ds(tap, 1), lanes]
                    acc = part if acc is None else acc + part
            rows = pl.ds(c * CH, CH)
            if base is not None:
                acc = acc + base[rows, lanes]
            out_ref[rows, lanes] = acc


def conv_taps_grad(s_ref, d_ref, extent, store):
    radius = extent // 2
    for half in range(2):
        lanes = pl.ds(half * 128, 128)
        sums = [None] * (extent * extent)
        for c in range(ROWS // CH):
            d = d_ref[pl.ds(c * CH, CH), lanes]
            for a in range(extent):
                for b in range(extent):
                    part = s_ref[b, pl.ds(32 + c * CH + 16 * (a - radius), CH), lanes] * d
                    part = jnp.sum(part.reshape(CH // 8, 8, 128), axis=0)
                    tap = a * extent + b
                    sums[tap] = part if sums[tap] is None else sums[tap] + part
        for tap, s in enumerate(sums):
            store(tap, lanes, jnp.sum(s, axis=0, keepdims=True))


def head_keys(half):
    lane = iota((1, 128), 1)
    parts = []
    for hh in range(4):
        own = (lane >= hh * HD) & (lane < (hh + 1) * HD)
        parts.append(jnp.where(own, half, jnp.zeros_like(half)))
    return jnp.concatenate(parts, 0)


def gelu_pair(x):
    cdf = 0.5 * (1.0 + lax.erf(x * (2.0**-0.5)))
    pdf = jnp.exp2(x * x * (-0.5 * LOG2E)) * (1.0 / math.sqrt(2.0 * math.pi))
    return x * cdf, cdf + x * pdf


class K:
    pass


def attn_fwd(l, k):
    x = k.x[...]
    shifted_into(k.sx.at[l], x, 3)
    conv_from(k.sx.at[l], k.posf.at[l], 3, False, k.x, k.tmp)
    mixed = k.tmp[...]
    xhat, rstd = norm_parts(mixed)
    k.a_xhat[l] = xhat
    k.a_rstd[l] = rstd
    gain = k.againf[pl.ds(l, 1), :]
    bias = k.abiasf[pl.ds(l, 1), :]
    normed = jnp.where(keep_rows(), xhat * gain + bias, 0.0).astype(BF16)
    k.a_normed[l] = normed
    k.need(l, "qkv")
    packed = nn(normed, k.qkv[l]).astype(BF16)
    q = packed[:, :D]
    key = packed[:, D : 2 * D]
    val = packed[:, 2 * D :]
    k.key[l] = key
    k.val[l] = val
    zpad = jnp.zeros((FULL - ROWS, D), BF16)
    qT, kT, vT = (jnp.concatenate([part, zpad], 0).T for part in (q, key, val))
    k.qT[l] = qT
    k.kT[l] = kT
    shifted_into(k.sv.at[l], val.astype(F32), 5)
    conv_from(k.sv.at[l], k.lepef.at[l], 5, False, None, k.tmp2)
    eqT = k.eqT[...]
    c = HD**-0.5 * LOG2E
    zkeys = jnp.zeros((FULL - ROWS, FULL), BF16)
    outs, scores = [], []
    for half in range(2):
        lanes = slice(half * 128, half * 128 + 128)
        heads = pl.ds(l * HEADS + half * 4, 4)
        rhs = jnp.concatenate([qT[lanes], eqT], 0)
        lhs = jnp.concatenate([head_keys(key[:, lanes]), k.blocked[heads].reshape(4 * ROWS, 128)], 1)
        scores.append(nn(lhs, rhs).reshape(4, ROWS, FULL))
    for half in range(2):
        heads = pl.ds(l * HEADS + half * 4, 4)
        s = scores[half]
        m = jnp.max(s, axis=1, keepdims=True)
        e = jnp.exp2((s - m) * c)
        r = 1.0 / jnp.sum(e, axis=1, keepdims=True)
        eb = e.astype(BF16)
        for hh in range(4):
            h = half * 4 + hh
            outs.append(nn(vT[h * HD : (h + 1) * HD], jnp.concatenate([eb[hh], zkeys], 0)) * r[hh])
        p = e * r
        k.p[heads] = p
        k.pb[heads, :ROWS] = p.astype(BF16)
    ctx = (jnp.concatenate(outs, 0).T[:ROWS] + k.tmp2[...]).astype(BF16)
    k.ctx[l] = ctx
    k.need(l, "proj")
    res = k.tmp[...] + nn(ctx, k.proj[l])
    k.x[...] = jnp.where(keep_rows(), res, 0.0).astype(BF16).astype(F32)


def mlp_fwd(l, k):
    x = k.x[...]
    xhat, rstd = norm_parts(x)
    k.m_xhat[l] = xhat
    k.m_rstd[l] = rstd
    normed = (xhat * k.mgainf[pl.ds(l, 1), :] + k.mbiasf[pl.ds(l, 1), :]).astype(BF16)
    k.m_normed[l] = normed
    k.need(l, "fc1")
    hidden = nn(normed, k.fc1[l])
    act, slope = gelu_pair(hidden)
    act = act.astype(BF16)
    k.act[l] = act
    k.slope[l] = slope
    k.need(l, "fc2")
    res = x + nn(act, k.fc2[l])
    k.x[...] = jnp.where(keep_rows(), res, 0.0).astype(BF16).astype(F32)


def norm_bwd(dy, xhat, rstd, gain, store_gain, store_bias):
    store_gain(jnp.sum(dy * xhat, axis=0, keepdims=True))
    store_bias(jnp.sum(dy, axis=0, keepdims=True))
    dg = dy * gain
    m1 = jnp.sum(dg, axis=-1, keepdims=True) * (1.0 / D)
    m2 = jnp.sum(dg * xhat, axis=-1, keepdims=True) * (1.0 / D)
    return rstd * (dg - m1 - xhat * m2)


def mlp_bwd_fc2(l, k):
    k.store("fc2", l, tn(k.act[l], k.g[...].astype(BF16)))


def mlp_bwd(l, k):
    g = k.g[...]
    gb = g.astype(BF16)
    dact = nt(gb, k.fc2[l]).astype(BF16).astype(F32)
    dhid = (k.slope[l] * dact).astype(BF16)
    k.store("fc1", l, tn(k.m_normed[l], dhid))
    dn = nt(dhid, k.fc1[l]).astype(BF16).astype(F32)
    dx = norm_bwd(
        dn,
        k.m_xhat[l],
        k.m_rstd[l],
        k.mgainf[pl.ds(l, 1), :],
        lambda v: k.store_row("mgain", l, 0, slice(None), v),
        lambda v: k.store_row("mbias", l, 0, slice(None), v),
    )
    k.g[...] = (dx + g).astype(BF16).astype(F32)


def attn_bwd_start(l, k):
    g = k.g[...]
    gb = g.astype(BF16)
    k.store("proj", l, tn(k.ctx[l], gb))
    dctx = nt(gb, k.proj[l]).astype(BF16)
    dctx32 = dctx.astype(F32)
    k.dctx[l] = dctx32
    zpad = jnp.zeros((FULL - ROWS, D), BF16)
    k.dcT[...] = jnp.concatenate([dctx, zpad], 0).T
    shifted_into(k.sd, dctx32, 5)


def attn_bwd_lepe(l, k):
    conv_taps_grad(k.sv.at[l], k.dctx.at[l], 5, lambda tap, lanes, v: k.store_row("lepe", l, tap, lanes, v))


def attn_bwd_conv(l, k):
    conv_from(k.sd, k.lepef.at[l], 5, True, None, k.tmp2)


def attn_bwd_heads(l, k):
    scale = HD**-0.5
    zkeys = jnp.zeros((FULL - ROWS, FULL), BF16)
    grads = []
    for half in range(2):
        lanes = slice(half * 128, half * 128 + 128)
        grads.append(nn(head_keys(k.val[l, :, lanes]), k.dcT[lanes]).reshape(4, ROWS, FULL))
    dq, dk, dv = [], [], []
    for half in range(2):
        p = k.p[pl.ds(l * HEADS + half * 4, 4)]
        pd = p * grads[half]
        ds = (pd - p * jnp.sum(pd, axis=1, keepdims=True)).astype(BF16)
        for hh in range(4):
            h = half * 4 + hh
            rows = slice(h * HD, (h + 1) * HD)
            dsb = jnp.concatenate([ds[hh], zkeys], 0)
            dv.append(nt(k.dcT[rows], k.pb[l * HEADS + h]))
            dq.append(nn(k.kT[l, rows], dsb))
            dk.append(nt(k.qT[l, rows], dsb))
    dq, dk, dv = (jnp.concatenate(part, 0).T[:ROWS] for part in (dq, dk, dv))
    dq = (dq * scale).astype(BF16)
    dk = (dk * scale).astype(BF16)
    dv = jnp.where(keep_rows(), dv + k.tmp2[...], 0.0).astype(BF16)
    dpacked = jnp.concatenate([dq, dk, dv], 1)
    k.dpacked[...] = dpacked
    k.store("qkv", l, tn(k.a_normed[l], dpacked))


def attn_bwd_end(l, k):
    g = k.g[...]
    dn = nt(k.dpacked[...], k.qkv[l]).astype(BF16).astype(F32)
    dx = norm_bwd(
        dn,
        k.a_xhat[l],
        k.a_rstd[l],
        k.againf[pl.ds(l, 1), :],
        lambda v: k.store_row("again", l, 0, slice(None), v),
        lambda v: k.store_row("abias", l, 0, slice(None), v),
    )
    dmixed = dx + g
    k.dmixed[l] = dmixed


def attn_bwd_pos(l, k):
    conv_taps_grad(k.sx.at[l], k.dmixed.at[l], 3, lambda tap, lanes, v: k.store_row("pos", l, tap, lanes, v))


def attn_bwd_input(l, k):
    shifted_into(k.sd, k.dmixed[l], 3)
    conv_from(k.sd, k.posf.at[l], 3, True, k.dmixed.at[l], k.tmp2)
    k.g[...] = jnp.where(keep_rows(), k.tmp2[...], 0.0).astype(BF16).astype(F32)


def prepare(k, tok, cot, routes):
    t = iota((ROWS, TOKS), 0)
    spread = ((t >> 4) * SIDE + (t & 15) == iota((ROWS, TOKS), 1)) & valid(t)
    spread = spread.astype(F32).astype(BF16)
    k.x[...] = nn(spread, tok)
    k.g[...] = nn(spread, cot)
    t = iota((ROWS, 128), 0)
    reg = jnp.where(valid(t), region_of(t), REGIONS)
    k.ekey[...] = (reg == iota((ROWS, 128), 1)).astype(F32).astype(BF16)
    t = iota((128, FULL), 1)
    k.eqT[...] = ((region_of(t) == iota((128, FULL), 0)) & valid(t)).astype(F32).astype(BF16)
    place = iota((128, REGIONS), 0)
    k.open[...] = jnp.zeros_like(k.open)
    k.pb[:, ROWS:, :] = jnp.zeros((k.pb.shape[0], FULL - ROWS, FULL), BF16)
    for ref in (k.sx, k.sv):
        for l in range(ref.shape[0]):
            for b in range(ref.shape[1]):
                ref[l, b, :32] = jnp.zeros((32, D), F32)
                ref[l, b, 32 + ROWS :] = jnp.zeros((32, D), F32)
    for b in range(5):
        k.sd[b, :32] = jnp.zeros((32, D), F32)
        k.sd[b, 32 + ROWS :] = jnp.zeros((32, D), F32)
    ekey = k.ekey[...]
    for lh in range(k.blocked.shape[0]):
        hit = None
        for j in range(TOPK):
            same = routes[lh // HEADS, lh % HEADS, pl.ds(j, 1), :] == place
            hit = same if hit is None else hit | same
        k.open[lh, :, :REGIONS] = jnp.where(hit, 0.0, BLOCKED).astype(BF16)
    for lh in range(0, k.blocked.shape[0], 2):
        both = nn(ekey, jnp.concatenate([k.open[lh], k.open[lh + 1]], 1)).astype(BF16)
        k.blocked[lh] = both[:, :128]
        k.blocked[lh + 1] = both[:, 128:]
    k.againf[:k.again.shape[0], :] = k.again[...].astype(F32)
    k.abiasf[:k.abias.shape[0], :] = k.abias[...].astype(F32)
    k.mgainf[:k.mgain.shape[0], :] = k.mgain[...].astype(F32)
    k.mbiasf[:k.mbias.shape[0], :] = k.mbias[...].astype(F32)
    for tap in range(9):
        k.posf[:, tap, :] = k.pos[tap].astype(F32)
    for tap in range(25):
        k.lepef[:, tap, :] = k.lepe[tap].astype(F32)


def scratch(layers):
    one = pltpu.VMEM
    return dict(
        againf=one((8, D), F32),
        abiasf=one((8, D), F32),
        mgainf=one((8, D), F32),
        mbiasf=one((8, D), F32),
        posf=one((layers, 16, D), F32),
        lepef=one((layers, 32, D), F32),
        x=one((ROWS, D), F32),
        g=one((ROWS, D), F32),
        tmp=one((ROWS, D), F32),
        tmp2=one((ROWS, D), F32),
        sx=one((layers, 3, 64 + ROWS, D), F32),
        sv=one((layers, 5, 64 + ROWS, D), F32),
        sd=one((5, 64 + ROWS, D), F32),
        a_xhat=one((layers, ROWS, D), F32),
        a_rstd=one((layers, ROWS, 1), F32),
        a_normed=one((layers, ROWS, D), BF16),
        key=one((layers, ROWS, D), BF16),
        val=one((layers, ROWS, D), BF16),
        qT=one((layers, D, FULL), BF16),
        kT=one((layers, D, FULL), BF16),
        dcT=one((D, FULL), BF16),
        dpacked=one((ROWS, 3 * D), BF16),
        dctx=one((layers, ROWS, D), F32),
        dmixed=one((layers, ROWS, D), F32),
        p=one((layers * HEADS, ROWS, FULL), F32),
        pb=one((layers * HEADS, FULL, FULL), BF16),
        blocked=one((layers * HEADS, ROWS, 128), BF16),
        open=one((layers * HEADS, 128, 128), BF16),
        ekey=one((ROWS, 128), BF16),
        eqT=one((128, FULL), BF16),
        ctx=one((layers, ROWS, D), BF16),
        m_xhat=one((layers, ROWS, D), F32),
        m_rstd=one((layers, ROWS, 1), F32),
        m_normed=one((layers, ROWS, D), BF16),
        act=one((layers, ROWS, 3 * D), BF16),
        slope=one((layers, ROWS, 3 * D), F32),
    )


class Group:
    def __init__(self, where, axis, stride, size, index=None):
        self.where, self.axis, self.stride, self.size = where, axis, stride, size
        self.index = (where[axis] // stride) % size if index is None else index

    def member(self, j):
        at = list(self.where)
        at[self.axis] = self.where[self.axis] + (j - self.index) * self.stride
        return tuple(at)

    def after(self, step):
        return lax.rem(self.index + step, self.size)


class Exchange:
    def __init__(self, mine, total, base, rows, groups, bufs, send, recv):
        self.mine, self.total, self.groups = mine, total, groups
        self.bufs, self.send, self.recv = bufs, send, recv
        self.base, self.rows = [base], [rows]
        for group, split in groups:
            size = self.rows[-1] // group.size if split else self.rows[-1]
            self.rows.append(size)
            self.base.append(self.base[-1] + group.index * size if split else self.base[-1])
        self.flight, self.owed = None, []

    def part(self, stage, j):
        size = self.rows[stage + 1]
        return pl.ds(pl.multiple_of(self.base[stage] + j * size, 16), size)

    def own(self, stage):
        return pl.ds(pl.multiple_of(self.base[stage], 16), self.rows[stage])

    def copy(self, sem, src, dst, to):
        return pltpu.make_async_remote_copy(
            src_ref=src,
            dst_ref=dst,
            send_sem=self.send.at[sem],
            recv_sem=self.recv.at[sem],
            device_id=to,
            device_id_type=pl.DeviceIdType.MESH,
        )

    def started(self, sem, like):
        self.flight = self.copy(sem, like, like, self.groups[0][0].member(self.groups[0][0].after(1)))
        self.owed.append(self.flight)

    def go(self, stage):
        group, split = self.groups[stage]
        sem, buf = self.bufs[stage]
        others = group.size - 1
        if not split:
            buf[group.index] = self.mine[self.own(stage), :]
        for step in range(1, group.size):
            to = group.after(step)
            if split:
                src, dst = self.mine.at[self.part(stage, to), :], buf.at[step - 1]
            else:
                src, dst = self.mine.at[self.own(stage), :], buf.at[group.index]
            self.copy(sem, src, dst, group.member(to)).start()
        self.started(sem, buf if split else buf.at[pl.ds(0, others)])

    def add(self, stage):
        group, split = self.groups[stage]
        _, buf = self.bufs[stage]
        if not split:
            self.owed.pop().wait_send()
        self.flight.wait_recv()
        mine = self.own(stage + 1)
        last = stage + 1 == len(self.groups)
        to = self.total if last else self.mine
        if split:
            total = self.mine[mine, :].astype(F32)
            for step in range(group.size - 1):
                total = total + buf[step].astype(F32)
        else:
            total = buf[0].astype(F32)
            for j in range(1, group.size):
                total = total + buf[j].astype(F32)
        to[mine, :] = total.astype(BF16)

    def back(self, stage):
        group, _ = self.groups[stage]
        sem = self.bufs[stage][0] + 1
        rows = self.part(stage, group.index)
        for step in range(1, group.size):
            self.copy(sem, self.total.at[rows, :], self.total.at[rows, :], group.member(group.after(step))).start()
        others = (group.size - 1) * self.rows[stage + 1]
        self.started(sem, self.total.at[pl.ds(pl.multiple_of(self.base[stage], 16), others), :])

    def steps(self):
        last = len(self.groups) - 1
        for stage in range(last + 1):
            self.go(stage)
            yield
            self.add(stage)
        ways = [stage for stage in range(last, -1, -1) if self.groups[stage][1]]
        for stage in ways:
            self.back(stage)
            yield
            if stage == ways[-1]:
                for sent in self.owed:
                    sent.wait_send()
            self.flight.wait_recv()


def groups_of(where, sections, dps):
    assert sections == 4 and dps % 8 == 0
    core = where[1] % 2
    low, high = where[0] % 2, where[0] // 2
    return {
        "c": Group(where, 1, 1, 2),
        "x": Group(where, 0, 1, 2),
        "y": Group(where, 0, 2, 2),
        "p": Group(where, 0, 1, 4),
        "u": Group(where, 0, 1 + core, 2, low + core * (high - low)),
        "v": Group(where, 0, 2 - core, 2, high + core * (low - high)),
        "z": Group(where, 1, 2, 2),
        "w": Group(where, 1, 4, 2),
        "q": Group(where, 1, 2, 4),
        "r": Group(where, 1, 8, dps // 8),
    }


IN_NAMES = ("tok", "routes", "pos", "again", "abias", "qkv", "lepe", "proj", "mgain", "mbias", "fc1", "fc2", "cot")
G_NAMES = ("pos", "again", "abias", "qkv", "lepe", "proj", "mgain", "mbias", "fc1", "fc2")

LAST = 80
LANES = 128

PIECES = (
    (1536, "cpq"),
    (1536, "cpq"),
    (2048, "czpW"),
    (1536, "cpq"),
    (1536, "cpq"),
    (512, "cpq"),
    (1536, "cpq"),
    (160, "cPQ"),
)
ORDER = (
    "wait", "a1", 0, "b1", 1, "s1", 0, "c1", 1, "h1", "k1", 2, "e1", "i1", "a0", 2, 3, "b0", 0, 3, 4,
    "s0", 5, "c0", "h0", 1, 4, 5, "k0", 2, 6, "e0", "i0", "grad", 0, 3, 6, 1, "l1", "p1", "l0", "p0",
    "last", "out", 4, 7, 5, 7, 2, 3, 0, 1, 6, 4, 5, 7, 2, 3, 0, 6, 0, 4, 1, 1, 2, 5, 7, 7, 6, 3, 3, 4, 5,
    4, 5, 2, 6, 2, 6,
)


def row_map(layers):
    at, n = {}, 0
    for l in reversed(range(layers)):
        for name, rows in (("fc2", 6 * D), ("fc1", 6 * D), ("proj", 2 * D), ("qkv", 6 * D)):
            at[name, l] = n
            n += rows
    at["last"] = n
    return at, n + 2 * LAST


def small_map(layers):
    at, n = {}, 0
    for l in reversed(range(layers)):
        for name, rows in (("pos", 9), ("again", 1), ("abias", 1), ("lepe", 25), ("mgain", 1), ("mbias", 1)):
            at[name, l] = n
            n += rows
    assert n <= LAST
    return at


def pieces_of(layers):
    assert layers == 2
    pieces, n = [], 0
    for rows, way in PIECES:
        pieces.append((n, rows, way))
        n += rows
    assert n == row_map(layers)[1]
    return pieces


def plan(where, sections, dps, layers):
    kinds = groups_of(where, sections, dps)
    pieces = pieces_of(layers)
    plans = []
    for base, rows, way in pieces:
        if kinds["r"].size > 1:
            way += "R"
        plans.append((base, rows, [(kinds[letter.lower()], letter.islower()) for letter in way]))
    return plans


def plan_buffers(plans):
    shapes, sems = [], 0
    where = []
    for base, rows, groups in plans:
        mine = []
        for group, split in groups:
            if split:
                rows //= group.size
                shapes.append(pltpu.VMEM((group.size - 1, rows, LANES), BF16))
                mine.append((sems, len(shapes) - 1))
                sems += 2
            else:
                shapes.append(pltpu.VMEM((group.size, rows, LANES), BF16))
                mine.append((sems, len(shapes) - 1))
                sems += 1
        where.append(mine)
    return shapes, sems, where


def body(layers, sections, dps, names, *refs):
    k = K()
    n_in = len(IN_NAMES)
    given = dict(zip(IN_NAMES, refs[:n_in]))
    out_ref, gin_ref, total = refs[n_in : n_in + 3]
    refs = refs[n_in + 3 :]
    for name, ref in zip(names, refs):
        setattr(k, name, ref)
    refs = refs[len(names) :]
    load = refs[n_in]
    loads = {}
    for i, name in enumerate(IN_NAMES):
        setattr(k, name, refs[i])
        loads[name] = pltpu.make_async_copy(given[name], refs[i], load.at[i])
    for name in LOAD_ORDER:
        loads[name].start()
    mine, last, send, recv = refs[n_in + 1 : n_in + 5]
    bufs = refs[n_in + 5 :]

    where = (lax.axis_index("section"), lax.axis_index("dp"))
    plans = plan(where, sections, dps, layers)
    _, _, slots = plan_buffers(plans)
    barrier = pltpu.get_barrier_semaphore()
    partners = 0
    kinds = groups_of(where, sections, dps)
    for kind in "cpqr":
        group = kinds[kind]
        for step in range(1, group.size):
            pl.semaphore_signal(barrier, inc=1, device_id=group.member(group.after(step)), device_id_type=pl.DeviceIdType.MESH)
            partners += 1

    at, _ = row_map(layers)
    small_at = small_map(layers)

    def need(l, name):
        if l == 0:
            loads[name].wait()

    def store(name, l, v):
        n = at[name, l]
        v = v.astype(BF16)
        height = v.shape[0]
        for c in range(v.shape[1] // LANES):
            mine[pl.ds(n + c * height, height), :] = v[:, c * LANES : (c + 1) * LANES]

    def store_row(name, l, tap, lanes, v):
        last[pl.ds(small_at[name, l] + tap, 1), lanes] = v

    def flush(ref, n):
        for c in range(2):
            mine[pl.ds(n + c * ref.shape[0], ref.shape[0]), :] = ref[:, c * LANES : (c + 1) * LANES].astype(BF16)

    k.need = need
    k.store = store
    k.store_row = store_row
    last[...] = jnp.zeros_like(last)
    for name in LOAD_ORDER:
        if name not in LATE:
            loads[name].wait()
    prepare(k, k.tok[0, 0], k.cot[0, 0], k.routes.at[0, 0])

    for l in range(layers):
        attn_fwd(l, k)
        mlp_fwd(l, k)
    t = iota((TOKS, ROWS), 1)
    gathered = ((t >> 4) * SIDE + (t & 15) == iota((TOKS, ROWS), 0)) & valid(t)
    gathered = gathered.astype(F32).astype(BF16)

    moves = []
    for (base, rows, groups), slot in zip(plans, slots):
        moves.append(
            Exchange(mine, total, base, rows, groups, [(sem, bufs[n]) for sem, n in slot], send, recv).steps()
        )

    def finish_out():
        out_ref[0, 0] = nn(gathered, k.x[...].astype(BF16)).astype(BF16)

    def finish_grad():
        gin_ref[0, 0] = nn(gathered, k.g[...].astype(BF16)).astype(BF16)

    work = {
        "wait": lambda: pl.semaphore_wait(barrier, partners),
        "out": finish_out,
        "grad": finish_grad,
        "last": lambda: flush(last, at["last"]),
    }
    for l in range(layers):
        for name, run in (
            ("a", mlp_bwd_fc2),
            ("b", mlp_bwd),
            ("s", attn_bwd_start),
            ("l", attn_bwd_lepe),
            ("c", attn_bwd_conv),
            ("h", attn_bwd_heads),
            ("k", lambda l, k: None),
            ("e", attn_bwd_end),
            ("i", attn_bwd_input),
            ("p", attn_bwd_pos),
        ):
            work[name + str(l)] = partial(run, l, k)
    for item in ORDER:
        if item in work:
            work[item]()
        else:
            next(moves[item], None)
    live = list(moves)
    while live:
        for m in list(live):
            if next(m, live) is live:
                live.remove(m)


def finish_body(layers, total, out_in, gin_in, *refs):
    outs = refs[:12]
    made = refs[12:24]
    sems = refs[24]
    at, _ = row_map(layers)
    small_at = small_map(layers)
    copies = []

    def go(src, dst):
        copy = pltpu.make_async_copy(src, dst, sems.at[len(copies)])
        copy.start()
        copies.append(copy)

    go(out_in, outs[0])
    go(gin_in, outs[1])
    places = dict(zip(G_NAMES, range(2, 12)))

    def wide(name, l, parts):
        ref = made[places[name]]
        for n, rows, top, col in parts:
            ref[l, pl.ds(top, rows), pl.ds(col, LANES)] = total[pl.ds(n, rows), :].astype(F32)
        go(ref.at[l], outs[places[name]].at[l])

    for l in reversed(range(layers)):
        wide("fc2", l, [(at["fc2", l] + c * 3 * D, 3 * D, 0, c * LANES) for c in range(2)])
        wide("fc1", l, [(at["fc1", l] + c * D, D, 0, c * LANES) for c in range(6)])
        wide("proj", l, [(at["proj", l] + c * D, D, 0, c * LANES) for c in range(2)])
        wide("qkv", l, [(at["qkv", l] + c * D, D, 0, c * LANES) for c in range(6)])

    def rows_from(n, count):
        return [total[pl.ds(n + c * count, count), :].astype(F32) for c in range(2)]

    both = rows_from(at["last"], LAST)
    for name, count in (("pos", 9), ("lepe", 25), ("again", 1), ("abias", 1), ("mgain", 1), ("mbias", 1)):
        ref = made[places[name]]
        for l in range(layers):
            n = small_at[name, l]
            for c in range(2):
                lanes = pl.ds(c * LANES, LANES)
                if count == 1:
                    ref[pl.ds(l, 1), lanes] = both[c][n : n + 1]
                else:
                    for tap in range(count):
                        ref[tap, pl.ds(l, 1), lanes] = both[c][n + tap : n + tap + 1]
        go(ref, outs[places[name]])
    for copy in copies:
        copy.wait()


LOAD_ORDER = ("tok", "routes", "cot", "pos", "again", "abias", "lepe", "mgain", "mbias", "qkv", "proj", "fc1", "fc2")
LATE = ("qkv", "proj", "fc1", "fc2")


def per_device(sections, dps, tokens, routes, pos, again, abias, qkv, lepe, proj, mgain, mbias, fc1, fc2, cot):
    layers = pos.shape[0]
    assert tokens.shape == (1, 1, TOKS, D)
    sc = scratch(layers)
    pos_t, lepe_t = (jnp.transpose(a, (1, 0, 2)) for a in (pos, lepe))
    routes_t = jnp.swapaxes(routes, -1, -2)
    args = (tokens, routes_t, pos_t, again, abias, qkv, lepe_t, proj, mgain, mbias, fc1, fc2, cot)
    vm = pl.BlockSpec(memory_space=pltpu.VMEM)
    hbm = pl.BlockSpec(memory_space=pl.ANY)
    _, count = row_map(layers)
    shapes, sems, _ = plan_buffers(plan((0, 0), sections, dps, layers))
    params = pltpu.CompilerParams(vmem_limit_bytes=58 * 2**20, collective_id=0, has_side_effects=True)
    out, gin, total = pl.pallas_call(
        partial(body, layers, sections, dps, tuple(sc)),
        out_shape=[pltpu.VMEM(tokens.shape, BF16)] * 2 + [pltpu.VMEM((count, LANES), BF16)],
        in_specs=[hbm] * len(args),
        out_specs=[vm] * 3,
        scratch_shapes=list(sc.values())
        + [pltpu.VMEM(a.shape, a.dtype) for a in args]
        + [
            pltpu.SemaphoreType.DMA((len(args),)),
            pltpu.VMEM((count, LANES), BF16),
            pltpu.VMEM((LAST, D), F32),
            pltpu.SemaphoreType.DMA((sems,)),
            pltpu.SemaphoreType.DMA((sems,)),
        ]
        + shapes,
        compiler_params=params,
        name="blocks",
    )(*args)
    weights = (pos_t, again, abias, qkv, lepe_t, proj, mgain, mbias, fc1, fc2)
    shapes = [jax.ShapeDtypeStruct(tokens.shape, BF16)] * 2 + [jax.ShapeDtypeStruct(w.shape, F32) for w in weights]
    res = pl.pallas_call(
        partial(finish_body, layers),
        out_shape=shapes,
        in_specs=[vm] * 3,
        out_specs=[hbm] * 12,
        scratch_shapes=[pltpu.VMEM(a.shape, a.dtype) for a in shapes] + [pltpu.SemaphoreType.DMA((2 + 4 * layers + 6,))],
        compiler_params=pltpu.CompilerParams(vmem_limit_bytes=32 * 2**20),
        name="widen",
    )(total, out, gin)
    res = list(res)
    res[2] = jnp.transpose(res[2], (1, 0, 2))
    res[6] = jnp.transpose(res[6], (1, 0, 2))
    return tuple(res)


def solution(mesh):
    image = P("section", "dp", None, None)
    sections, dps = mesh.shape["section"], mesh.shape["dp"]
    return jax.shard_map(
        partial(per_device, sections, dps),
        mesh=mesh,
        in_specs=(image, P("section", "dp", None, None, None, None)) + (P(),) * 10 + (image,),
        out_specs=(image, image) + (P(),) * 10,
        check_vma=False,
    )
```

```python
from functools import partial
import math

import jax
import jax.numpy as jnp
from jax import lax
from jax.experimental import pallas as pl
from jax.experimental.pallas import tpu as pltpu
from jax.sharding import PartitionSpec as P

F32 = jnp.float32
BF16 = jnp.bfloat16
EPS = 1e-06
HEADS = 8
SIDE = 14
WIDE = 16
TOKS = SIDE * SIDE
ROWS = SIDE * WIDE
FULL = 256
D = 256
HD = 32
REGIONS = 49
TOPK = 4
BLOCKED = -1e30
LOG2E = 1.4426950408889634


def nn(a, b):
    return lax.dot_general(a, b, (((1,), (0,)), ((), ())), preferred_element_type=F32)


def nt(a, b):
    return lax.dot_general(a, b, (((1,), (1,)), ((), ())), preferred_element_type=F32)


def tn(a, b):
    return lax.dot_general(a, b, (((0,), (0,)), ((), ())), preferred_element_type=F32)


def iota(shape, dim):
    return lax.broadcasted_iota(jnp.int32, shape, dim)


def region_of(t):
    return (t >> 5) * (SIDE // 2) + ((t & 15) >> 1)


def valid(t):
    return ((t & 15) < SIDE) & (t < ROWS)


def keep_rows():
    return valid(iota((ROWS, 1), 0))


def norm_parts(v):
    mean = jnp.sum(v, axis=-1, keepdims=True) * (1.0 / D)
    cen = v - mean
    var = jnp.sum(cen * cen, axis=-1, keepdims=True) * (1.0 / D)
    rstd = lax.rsqrt(var + EPS)
    return cen * rstd, rstd


def shifted_into(s_ref, x, extent):
    radius = extent // 2
    for b in range(extent):
        away = b - radius
        s_ref[b, pl.ds(32, ROWS), :] = x if away == 0 else pltpu.roll(x, (-away) % ROWS, 0)


CH = 112


def conv_from(s_ref, taps, extent, flip, base, out_ref):
    radius = extent // 2
    for half in range(2):
        lanes = pl.ds(half * 128, 128)
        for c in range(ROWS // CH):
            acc = None
            for a in range(extent):
                for b in range(extent):
                    tap = a * extent + b
                    if flip:
                        tap = extent * extent - 1 - tap
                    part = s_ref[b, pl.ds(32 + c * CH + 16 * (a - radius), CH), lanes]
                    part = part * taps[pl.ds(tap, 1), lanes]
                    acc = part if acc is None else acc + part
            rows = pl.ds(c * CH, CH)
            if base is not None:
                acc = acc + base[rows, lanes]
            out_ref[rows, lanes] = acc


def conv_taps_grad(s_ref, d_ref, extent, store):
    radius = extent // 2
    for half in range(2):
        lanes = pl.ds(half * 128, 128)
        sums = [None] * (extent * extent)
        for c in range(ROWS // CH):
            d = d_ref[pl.ds(c * CH, CH), lanes]
            for a in range(extent):
                for b in range(extent):
                    part = s_ref[b, pl.ds(32 + c * CH + 16 * (a - radius), CH), lanes] * d
                    part = jnp.sum(part.reshape(CH // 8, 8, 128), axis=0)
                    tap = a * extent + b
                    sums[tap] = part if sums[tap] is None else sums[tap] + part
        for tap, s in enumerate(sums):
            store(tap, lanes, jnp.sum(s, axis=0, keepdims=True))


def head_keys(half):
    lane = iota((1, 128), 1)
    parts = []
    for hh in range(4):
        own = (lane >= hh * HD) & (lane < (hh + 1) * HD)
        parts.append(jnp.where(own, half, jnp.zeros_like(half)))
    return jnp.concatenate(parts, 0)


def gelu_pair(x):
    cdf = 0.5 * (1.0 + lax.erf(x * (2.0**-0.5)))
    pdf = jnp.exp2(x * x * (-0.5 * LOG2E)) * (1.0 / math.sqrt(2.0 * math.pi))
    return x * cdf, cdf + x * pdf


class K:
    pass


def attn_fwd(l, k):
    x = k.x[...]
    shifted_into(k.sx.at[l], x, 3)
    conv_from(k.sx.at[l], k.posf.at[l], 3, False, k.x, k.tmp)
    mixed = k.tmp[...]
    xhat, rstd = norm_parts(mixed)
    k.a_xhat[l] = xhat
    k.a_rstd[l] = rstd
    gain = k.againf[pl.ds(l, 1), :]
    bias = k.abiasf[pl.ds(l, 1), :]
    normed = jnp.where(keep_rows(), xhat * gain + bias, 0.0).astype(BF16)
    k.a_normed[l] = normed
    k.need(l, "qkv")
    packed = nn(normed, k.qkv[l]).astype(BF16)
    q = packed[:, :D]
    key = packed[:, D : 2 * D]
    val = packed[:, 2 * D :]
    k.key[l] = key
    k.val[l] = val
    zpad = jnp.zeros((FULL - ROWS, D), BF16)
    qT, kT, vT = (jnp.concatenate([part, zpad], 0).T for part in (q, key, val))
    k.qT[l] = qT
    k.kT[l] = kT
    shifted_into(k.sv.at[l], val.astype(F32), 5)
    conv_from(k.sv.at[l], k.lepef.at[l], 5, False, None, k.tmp2)
    eqT = k.eqT[...]
    c = HD**-0.5 * LOG2E
    zkeys = jnp.zeros((FULL - ROWS, FULL), BF16)
    outs, scores = [], []
    for half in range(2):
        lanes = slice(half * 128, half * 128 + 128)
        heads = pl.ds(l * HEADS + half * 4, 4)
        rhs = jnp.concatenate([qT[lanes], eqT], 0)
        lhs = jnp.concatenate([head_keys(key[:, lanes]), k.blocked[heads].reshape(4 * ROWS, 128)], 1)
        scores.append(nn(lhs, rhs).reshape(4, ROWS, FULL))
    for half in range(2):
        heads = pl.ds(l * HEADS + half * 4, 4)
        s = scores[half]
        m = jnp.max(s, axis=1, keepdims=True)
        e = jnp.exp2((s - m) * c)
        r = 1.0 / jnp.sum(e, axis=1, keepdims=True)
        eb = e.astype(BF16)
        for hh in range(4):
            h = half * 4 + hh
            outs.append(nn(vT[h * HD : (h + 1) * HD], jnp.concatenate([eb[hh], zkeys], 0)) * r[hh])
        p = e * r
        k.p[heads] = p
        k.pb[heads, :ROWS] = p.astype(BF16)
    ctx = (jnp.concatenate(outs, 0).T[:ROWS] + k.tmp2[...]).astype(BF16)
    k.ctx[l] = ctx
    k.need(l, "proj")
    res = k.tmp[...] + nn(ctx, k.proj[l])
    k.x[...] = jnp.where(keep_rows(), res, 0.0).astype(BF16).astype(F32)


def mlp_fwd(l, k):
    x = k.x[...]
    xhat, rstd = norm_parts(x)
    k.m_xhat[l] = xhat
    k.m_rstd[l] = rstd
    normed = (xhat * k.mgainf[pl.ds(l, 1), :] + k.mbiasf[pl.ds(l, 1), :]).astype(BF16)
    k.m_normed[l] = normed
    k.need(l, "fc1")
    hidden = nn(normed, k.fc1[l])
    act, slope = gelu_pair(hidden)
    act = act.astype(BF16)
    k.act[l] = act
    k.slope[l] = slope
    k.need(l, "fc2")
    res = x + nn(act, k.fc2[l])
    k.x[...] = jnp.where(keep_rows(), res, 0.0).astype(BF16).astype(F32)


def norm_bwd(dy, xhat, rstd, gain, store_gain, store_bias):
    store_gain(jnp.sum(dy * xhat, axis=0, keepdims=True))
    store_bias(jnp.sum(dy, axis=0, keepdims=True))
    dg = dy * gain
    m1 = jnp.sum(dg, axis=-1, keepdims=True) * (1.0 / D)
    m2 = jnp.sum(dg * xhat, axis=-1, keepdims=True) * (1.0 / D)
    return rstd * (dg - m1 - xhat * m2)


def mlp_bwd_fc2(l, k):
    k.store("fc2", l, tn(k.act[l], k.g[...].astype(BF16)))


def mlp_bwd(l, k):
    g = k.g[...]
    gb = g.astype(BF16)
    dact = nt(gb, k.fc2[l]).astype(BF16).astype(F32)
    dhid = (k.slope[l] * dact).astype(BF16)
    k.store("fc1", l, tn(k.m_normed[l], dhid))
    dn = nt(dhid, k.fc1[l]).astype(BF16).astype(F32)
    dx = norm_bwd(
        dn,
        k.m_xhat[l],
        k.m_rstd[l],
        k.mgainf[pl.ds(l, 1), :],
        lambda v: k.store_row("mgain", l, 0, slice(None), v),
        lambda v: k.store_row("mbias", l, 0, slice(None), v),
    )
    k.g[...] = (dx + g).astype(BF16).astype(F32)


def attn_bwd_start(l, k):
    g = k.g[...]
    gb = g.astype(BF16)
    k.store("proj", l, tn(k.ctx[l], gb))
    dctx = nt(gb, k.proj[l]).astype(BF16)
    dctx32 = dctx.astype(F32)
    k.dctx[l] = dctx32
    zpad = jnp.zeros((FULL - ROWS, D), BF16)
    k.dcT[...] = jnp.concatenate([dctx, zpad], 0).T
    shifted_into(k.sd, dctx32, 5)


def attn_bwd_lepe(l, k):
    conv_taps_grad(k.sv.at[l], k.dctx.at[l], 5, lambda tap, lanes, v: k.store_row("lepe", l, tap, lanes, v))


def attn_bwd_conv(l, k):
    conv_from(k.sd, k.lepef.at[l], 5, True, None, k.tmp2)


def attn_bwd_heads(l, k):
    scale = HD**-0.5
    zkeys = jnp.zeros((FULL - ROWS, FULL), BF16)
    grads = []
    for half in range(2):
        lanes = slice(half * 128, half * 128 + 128)
        grads.append(nn(head_keys(k.val[l, :, lanes]), k.dcT[lanes]).reshape(4, ROWS, FULL))
    dq, dk, dv = [], [], []
    for half in range(2):
        p = k.p[pl.ds(l * HEADS + half * 4, 4)]
        pd = p * grads[half]
        ds = (pd - p * jnp.sum(pd, axis=1, keepdims=True)).astype(BF16)
        for hh in range(4):
            h = half * 4 + hh
            rows = slice(h * HD, (h + 1) * HD)
            dsb = jnp.concatenate([ds[hh], zkeys], 0)
            dv.append(nt(k.dcT[rows], k.pb[l * HEADS + h]))
            dq.append(nn(k.kT[l, rows], dsb))
            dk.append(nt(k.qT[l, rows], dsb))
    dq, dk, dv = (jnp.concatenate(part, 0).T[:ROWS] for part in (dq, dk, dv))
    dq = (dq * scale).astype(BF16)
    dk = (dk * scale).astype(BF16)
    dv = jnp.where(keep_rows(), dv + k.tmp2[...], 0.0).astype(BF16)
    dpacked = jnp.concatenate([dq, dk, dv], 1)
    k.dpacked[...] = dpacked
    k.store("qkv", l, tn(k.a_normed[l], dpacked))


def attn_bwd_end(l, k):
    g = k.g[...]
    dn = nt(k.dpacked[...], k.qkv[l]).astype(BF16).astype(F32)
    dx = norm_bwd(
        dn,
        k.a_xhat[l],
        k.a_rstd[l],
        k.againf[pl.ds(l, 1), :],
        lambda v: k.store_row("again", l, 0, slice(None), v),
        lambda v: k.store_row("abias", l, 0, slice(None), v),
    )
    dmixed = dx + g
    k.dmixed[l] = dmixed


def attn_bwd_pos(l, k):
    conv_taps_grad(k.sx.at[l], k.dmixed.at[l], 3, lambda tap, lanes, v: k.store_row("pos", l, tap, lanes, v))


def attn_bwd_input(l, k):
    shifted_into(k.sd, k.dmixed[l], 3)
    conv_from(k.sd, k.posf.at[l], 3, True, k.dmixed.at[l], k.tmp2)
    k.g[...] = jnp.where(keep_rows(), k.tmp2[...], 0.0).astype(BF16).astype(F32)


def prepare(k, tok, cot, routes):
    t = iota((ROWS, TOKS), 0)
    spread = ((t >> 4) * SIDE + (t & 15) == iota((ROWS, TOKS), 1)) & valid(t)
    spread = spread.astype(F32).astype(BF16)
    k.x[...] = nn(spread, tok)
    k.g[...] = nn(spread, cot)
    t = iota((ROWS, 128), 0)
    reg = jnp.where(valid(t), region_of(t), REGIONS)
    k.ekey[...] = (reg == iota((ROWS, 128), 1)).astype(F32).astype(BF16)
    t = iota((128, FULL), 1)
    k.eqT[...] = ((region_of(t) == iota((128, FULL), 0)) & valid(t)).astype(F32).astype(BF16)
    place = iota((128, REGIONS), 0)
    k.open[...] = jnp.zeros_like(k.open)
    k.pb[:, ROWS:, :] = jnp.zeros((k.pb.shape[0], FULL - ROWS, FULL), BF16)
    for ref in (k.sx, k.sv):
        for l in range(ref.shape[0]):
            for b in range(ref.shape[1]):
                ref[l, b, :32] = jnp.zeros((32, D), F32)
                ref[l, b, 32 + ROWS :] = jnp.zeros((32, D), F32)
    for b in range(5):
        k.sd[b, :32] = jnp.zeros((32, D), F32)
        k.sd[b, 32 + ROWS :] = jnp.zeros((32, D), F32)
    ekey = k.ekey[...]
    for lh in range(k.blocked.shape[0]):
        hit = None
        for j in range(TOPK):
            same = routes[lh // HEADS, lh % HEADS, pl.ds(j, 1), :] == place
            hit = same if hit is None else hit | same
        k.open[lh, :, :REGIONS] = jnp.where(hit, 0.0, BLOCKED).astype(BF16)
    for lh in range(0, k.blocked.shape[0], 2):
        both = nn(ekey, jnp.concatenate([k.open[lh], k.open[lh + 1]], 1)).astype(BF16)
        k.blocked[lh] = both[:, :128]
        k.blocked[lh + 1] = both[:, 128:]
    k.againf[:k.again.shape[0], :] = k.again[...].astype(F32)
    k.abiasf[:k.abias.shape[0], :] = k.abias[...].astype(F32)
    k.mgainf[:k.mgain.shape[0], :] = k.mgain[...].astype(F32)
    k.mbiasf[:k.mbias.shape[0], :] = k.mbias[...].astype(F32)
    for tap in range(9):
        k.posf[:, tap, :] = k.pos[tap].astype(F32)
    for tap in range(25):
        k.lepef[:, tap, :] = k.lepe[tap].astype(F32)


def scratch(layers):
    one = pltpu.VMEM
    return dict(
        againf=one((8, D), F32),
        abiasf=one((8, D), F32),
        mgainf=one((8, D), F32),
        mbiasf=one((8, D), F32),
        posf=one((layers, 16, D), F32),
        lepef=one((layers, 32, D), F32),
        x=one((ROWS, D), F32),
        g=one((ROWS, D), F32),
        tmp=one((ROWS, D), F32),
        tmp2=one((ROWS, D), F32),
        sx=one((layers, 3, 64 + ROWS, D), F32),
        sv=one((layers, 5, 64 + ROWS, D), F32),
        sd=one((5, 64 + ROWS, D), F32),
        a_xhat=one((layers, ROWS, D), F32),
        a_rstd=one((layers, ROWS, 1), F32),
        a_normed=one((layers, ROWS, D), BF16),
        key=one((layers, ROWS, D), BF16),
        val=one((layers, ROWS, D), BF16),
        qT=one((layers, D, FULL), BF16),
        kT=one((layers, D, FULL), BF16),
        dcT=one((D, FULL), BF16),
        dpacked=one((ROWS, 3 * D), BF16),
        dctx=one((layers, ROWS, D), F32),
        dmixed=one((layers, ROWS, D), F32),
        p=one((layers * HEADS, ROWS, FULL), F32),
        pb=one((layers * HEADS, FULL, FULL), BF16),
        blocked=one((layers * HEADS, ROWS, 128), BF16),
        open=one((layers * HEADS, 128, 128), BF16),
        ekey=one((ROWS, 128), BF16),
        eqT=one((128, FULL), BF16),
        ctx=one((layers, ROWS, D), BF16),
        m_xhat=one((layers, ROWS, D), F32),
        m_rstd=one((layers, ROWS, 1), F32),
        m_normed=one((layers, ROWS, D), BF16),
        act=one((layers, ROWS, 3 * D), BF16),
        slope=one((layers, ROWS, 3 * D), F32),
    )


class Group:
    def __init__(self, where, axis, stride, size, index=None):
        self.where, self.axis, self.stride, self.size = where, axis, stride, size
        self.index = (where[axis] // stride) % size if index is None else index

    def member(self, j):
        at = list(self.where)
        at[self.axis] = self.where[self.axis] + (j - self.index) * self.stride
        return tuple(at)

    def after(self, step):
        if self.size != 4:
            return lax.rem(self.index + step, self.size)
        first = (3 - self.index, self.index + 1 - 2 * lax.rem(self.index, 2), self.index + 2 - 4 * (self.index // 2))
        second = (self.index + 1 - 2 * lax.rem(self.index, 2), self.index + 2 - 4 * (self.index // 2), 3 - self.index)
        return (first if self.axis == 0 else second)[step - 1]


class Exchange:
    def __init__(self, mine, total, base, rows, groups, bufs, send, recv):
        self.mine, self.total, self.groups = mine, total, groups
        self.bufs, self.send, self.recv = bufs, send, recv
        self.base, self.rows = [base], [rows]
        for group, split in groups:
            size = self.rows[-1] // group.size if split else self.rows[-1]
            self.rows.append(size)
            self.base.append(self.base[-1] + group.index * size if split else self.base[-1])
        self.flight, self.owed = None, []

    def part(self, stage, j):
        size = self.rows[stage + 1]
        return pl.ds(pl.multiple_of(self.base[stage] + j * size, 16), size)

    def own(self, stage):
        return pl.ds(pl.multiple_of(self.base[stage], 16), self.rows[stage])

    def copy(self, sem, src, dst, to):
        return pltpu.make_async_remote_copy(
            src_ref=src,
            dst_ref=dst,
            send_sem=self.send.at[sem],
            recv_sem=self.recv.at[sem],
            device_id=to,
            device_id_type=pl.DeviceIdType.MESH,
        )

    def started(self, sem, like):
        self.flight = self.copy(sem, like, like, self.groups[0][0].member(self.groups[0][0].after(1)))
        self.owed.append(self.flight)

    def go(self, stage):
        group, split = self.groups[stage]
        sem, buf = self.bufs[stage]
        others = group.size - 1
        if not split:
            buf[group.index] = self.mine[self.own(stage), :]
        for step in range(1, group.size):
            to = group.after(step)
            if split:
                src, dst = self.mine.at[self.part(stage, to), :], buf.at[step - 1]
            else:
                src, dst = self.mine.at[self.own(stage), :], buf.at[group.index]
            self.copy(sem, src, dst, group.member(to)).start()
        self.started(sem, buf if split else buf.at[pl.ds(0, others)])

    def add(self, stage):
        group, split = self.groups[stage]
        _, buf = self.bufs[stage]
        if not split:
            self.owed.pop().wait_send()
        self.flight.wait_recv()
        mine = self.own(stage + 1)
        last = stage + 1 == len(self.groups)
        to = self.total if last else self.mine
        if split:
            total = self.mine[mine, :].astype(F32)
            for step in range(group.size - 1):
                total = total + buf[step].astype(F32)
        else:
            total = buf[0].astype(F32)
            for j in range(1, group.size):
                total = total + buf[j].astype(F32)
        to[mine, :] = total.astype(BF16)

    def back(self, stage):
        group, _ = self.groups[stage]
        sem = self.bufs[stage][0] + 1
        rows = self.part(stage, group.index)
        for step in range(1, group.size):
            self.copy(sem, self.total.at[rows, :], self.total.at[rows, :], group.member(group.after(step))).start()
        others = (group.size - 1) * self.rows[stage + 1]
        self.started(sem, self.total.at[pl.ds(pl.multiple_of(self.base[stage], 16), others), :])

    def steps(self):
        last = len(self.groups) - 1
        for stage in range(last + 1):
            self.go(stage)
            yield
            self.add(stage)
        ways = [stage for stage in range(last, -1, -1) if self.groups[stage][1]]
        for stage in ways:
            self.back(stage)
            yield
            if stage == ways[-1]:
                for sent in self.owed:
                    sent.wait_send()
            self.flight.wait_recv()


def groups_of(where, sections, dps):
    assert sections == 4 and dps % 8 == 0
    core = where[1] % 2
    low, high = where[0] % 2, where[0] // 2
    return {
        "c": Group(where, 1, 1, 2),
        "x": Group(where, 0, 1, 2),
        "y": Group(where, 0, 2, 2),
        "p": Group(where, 0, 1, 4),
        "u": Group(where, 0, 1 + core, 2, low + core * (high - low)),
        "v": Group(where, 0, 2 - core, 2, high + core * (low - high)),
        "z": Group(where, 1, 2, 2),
        "w": Group(where, 1, 4, 2),
        "q": Group(where, 1, 2, 4),
        "r": Group(where, 1, 8, dps // 8),
    }


IN_NAMES = ("tok", "routes", "pos", "again", "abias", "qkv", "lepe", "proj", "mgain", "mbias", "fc1", "fc2", "cot")
G_NAMES = ("pos", "again", "abias", "qkv", "lepe", "proj", "mgain", "mbias", "fc1", "fc2")

LAST = 80
LANES = 128

PIECES = (
    (1536, "cpq"),
    (1536, "cpq"),
    (2048, "czpW"),
    (1536, "cpq"),
    (1536, "cpq"),
    (512, "cpq"),
    (1536, "cpq"),
    (160, "cPQ"),
)
ORDER = (
    "wait", "a1", 0, "b1", 1, "s1", 0, "c1", 1, "h1", "k1", 2, "e1", "i1", "a0", 2, 3, "b0", 0, 3, 4,
    "s0", 5, "c0", "h0", 1, 4, 5, "k0", 2, 6, "e0", "i0", "grad", 0, 3, 6, 1, "l1", "p1", "l0", "p0",
    "last", "out", 4, 7, 5, 7, 2, 3, 0, 1, 6, 4, 5, 7, 2, 3, 0, 6, 0, 4, 1, 1, 2, 5, 7, 7, 6, 3, 3, 4, 5,
    4, 5, 2, 6, 2, 6,
)


def row_map(layers):
    at, n = {}, 0
    for l in reversed(range(layers)):
        for name, rows in (("fc2", 6 * D), ("fc1", 6 * D), ("proj", 2 * D), ("qkv", 6 * D)):
            at[name, l] = n
            n += rows
    at["last"] = n
    return at, n + 2 * LAST


def small_map(layers):
    at, n = {}, 0
    for l in reversed(range(layers)):
        for name, rows in (("pos", 9), ("again", 1), ("abias", 1), ("lepe", 25), ("mgain", 1), ("mbias", 1)):
            at[name, l] = n
            n += rows
    assert n <= LAST
    return at


def pieces_of(layers):
    assert layers == 2
    pieces, n = [], 0
    for rows, way in PIECES:
        pieces.append((n, rows, way))
        n += rows
    assert n == row_map(layers)[1]
    return pieces


def plan(where, sections, dps, layers):
    kinds = groups_of(where, sections, dps)
    pieces = pieces_of(layers)
    plans = []
    for base, rows, way in pieces:
        if kinds["r"].size > 1:
            way += "R"
        plans.append((base, rows, [(kinds[letter.lower()], letter.islower()) for letter in way]))
    return plans


def plan_buffers(plans):
    shapes, sems = [], 0
    where = []
    for base, rows, groups in plans:
        mine = []
        for group, split in groups:
            if split:
                rows //= group.size
                shapes.append(pltpu.VMEM((group.size - 1, rows, LANES), BF16))
                mine.append((sems, len(shapes) - 1))
                sems += 2
            else:
                shapes.append(pltpu.VMEM((group.size, rows, LANES), BF16))
                mine.append((sems, len(shapes) - 1))
                sems += 1
        where.append(mine)
    return shapes, sems, where


def body(layers, sections, dps, names, *refs):
    k = K()
    n_in = len(IN_NAMES)
    given = dict(zip(IN_NAMES, refs[:n_in]))
    out_ref, gin_ref, total = refs[n_in : n_in + 3]
    refs = refs[n_in + 3 :]
    for name, ref in zip(names, refs):
        setattr(k, name, ref)
    refs = refs[len(names) :]
    load = refs[n_in]
    loads = {}
    for i, name in enumerate(IN_NAMES):
        setattr(k, name, refs[i])
        loads[name] = pltpu.make_async_copy(given[name], refs[i], load.at[i])
    for name in LOAD_ORDER:
        loads[name].start()
    mine, last, send, recv = refs[n_in + 1 : n_in + 5]
    bufs = refs[n_in + 5 :]

    where = (lax.axis_index("section"), lax.axis_index("dp"))
    plans = plan(where, sections, dps, layers)
    _, _, slots = plan_buffers(plans)
    barrier = pltpu.get_barrier_semaphore()
    partners = 0
    kinds = groups_of(where, sections, dps)
    for kind in "cpqr":
        group = kinds[kind]
        for step in range(1, group.size):
            pl.semaphore_signal(barrier, inc=1, device_id=group.member(group.after(step)), device_id_type=pl.DeviceIdType.MESH)
            partners += 1

    at, _ = row_map(layers)
    small_at = small_map(layers)

    def need(l, name):
        if l == 0:
            loads[name].wait()

    def store(name, l, v):
        n = at[name, l]
        v = v.astype(BF16)
        height = v.shape[0]
        for c in range(v.shape[1] // LANES):
            mine[pl.ds(n + c * height, height), :] = v[:, c * LANES : (c + 1) * LANES]

    def store_row(name, l, tap, lanes, v):
        last[pl.ds(small_at[name, l] + tap, 1), lanes] = v

    def flush(ref, n):
        for c in range(2):
            mine[pl.ds(n + c * ref.shape[0], ref.shape[0]), :] = ref[:, c * LANES : (c + 1) * LANES].astype(BF16)

    k.need = need
    k.store = store
    k.store_row = store_row
    last[...] = jnp.zeros_like(last)
    for name in LOAD_ORDER:
        if name not in LATE:
            loads[name].wait()
    prepare(k, k.tok[0, 0], k.cot[0, 0], k.routes.at[0, 0])

    for l in range(layers):
        attn_fwd(l, k)
        mlp_fwd(l, k)
    t = iota((TOKS, ROWS), 1)
    gathered = ((t >> 4) * SIDE + (t & 15) == iota((TOKS, ROWS), 0)) & valid(t)
    gathered = gathered.astype(F32).astype(BF16)

    moves = []
    for (base, rows, groups), slot in zip(plans, slots):
        moves.append(
            Exchange(mine, total, base, rows, groups, [(sem, bufs[n]) for sem, n in slot], send, recv).steps()
        )

    def finish_out():
        out_ref[0, 0] = nn(gathered, k.x[...].astype(BF16)).astype(BF16)

    def finish_grad():
        gin_ref[0, 0] = nn(gathered, k.g[...].astype(BF16)).astype(BF16)

    work = {
        "wait": lambda: pl.semaphore_wait(barrier, partners),
        "out": finish_out,
        "grad": finish_grad,
        "last": lambda: flush(last, at["last"]),
    }
    for l in range(layers):
        for name, run in (
            ("a", mlp_bwd_fc2),
            ("b", mlp_bwd),
            ("s", attn_bwd_start),
            ("l", attn_bwd_lepe),
            ("c", attn_bwd_conv),
            ("h", attn_bwd_heads),
            ("k", lambda l, k: None),
            ("e", attn_bwd_end),
            ("i", attn_bwd_input),
            ("p", attn_bwd_pos),
        ):
            work[name + str(l)] = partial(run, l, k)
    for item in ORDER:
        if item in work:
            work[item]()
        else:
            next(moves[item], None)
    live = list(moves)
    while live:
        for m in list(live):
            if next(m, live) is live:
                live.remove(m)


def finish_body(layers, total, out_in, gin_in, *refs):
    outs = refs[:12]
    made = refs[12:24]
    sems = refs[24]
    at, _ = row_map(layers)
    small_at = small_map(layers)
    copies = []

    def go(src, dst):
        copy = pltpu.make_async_copy(src, dst, sems.at[len(copies)])
        copy.start()
        copies.append(copy)

    go(out_in, outs[0])
    go(gin_in, outs[1])
    places = dict(zip(G_NAMES, range(2, 12)))

    def wide(name, l, parts):
        ref = made[places[name]]
        for n, rows, top, col in parts:
            ref[l, pl.ds(top, rows), pl.ds(col, LANES)] = total[pl.ds(n, rows), :].astype(F32)
        go(ref.at[l], outs[places[name]].at[l])

    for l in reversed(range(layers)):
        wide("fc2", l, [(at["fc2", l] + c * 3 * D, 3 * D, 0, c * LANES) for c in range(2)])
        wide("fc1", l, [(at["fc1", l] + c * D, D, 0, c * LANES) for c in range(6)])
        wide("proj", l, [(at["proj", l] + c * D, D, 0, c * LANES) for c in range(2)])
        wide("qkv", l, [(at["qkv", l] + c * D, D, 0, c * LANES) for c in range(6)])

    def rows_from(n, count):
        return [total[pl.ds(n + c * count, count), :].astype(F32) for c in range(2)]

    both = rows_from(at["last"], LAST)
    for name, count in (("pos", 9), ("lepe", 25), ("again", 1), ("abias", 1), ("mgain", 1), ("mbias", 1)):
        ref = made[places[name]]
        for l in range(layers):
            n = small_at[name, l]
            for c in range(2):
                lanes = pl.ds(c * LANES, LANES)
                if count == 1:
                    ref[pl.ds(l, 1), lanes] = both[c][n : n + 1]
                else:
                    for tap in range(count):
                        ref[tap, pl.ds(l, 1), lanes] = both[c][n + tap : n + tap + 1]
        go(ref, outs[places[name]])
    for copy in copies:
        copy.wait()


LOAD_ORDER = ("tok", "routes", "cot", "pos", "again", "abias", "lepe", "mgain", "mbias", "qkv", "proj", "fc1", "fc2")
LATE = ("qkv", "proj", "fc1", "fc2")


def per_device(sections, dps, tokens, routes, pos, again, abias, qkv, lepe, proj, mgain, mbias, fc1, fc2, cot):
    layers = pos.shape[0]
    assert tokens.shape == (1, 1, TOKS, D)
    sc = scratch(layers)
    pos_t, lepe_t = (jnp.transpose(a, (1, 0, 2)) for a in (pos, lepe))
    routes_t = jnp.swapaxes(routes, -1, -2)
    args = (tokens, routes_t, pos_t, again, abias, qkv, lepe_t, proj, mgain, mbias, fc1, fc2, cot)
    vm = pl.BlockSpec(memory_space=pltpu.VMEM)
    hbm = pl.BlockSpec(memory_space=pl.ANY)
    _, count = row_map(layers)
    shapes, sems, _ = plan_buffers(plan((0, 0), sections, dps, layers))
    params = pltpu.CompilerParams(vmem_limit_bytes=58 * 2**20, collective_id=0, has_side_effects=True)
    out, gin, total = pl.pallas_call(
        partial(body, layers, sections, dps, tuple(sc)),
        out_shape=[pltpu.VMEM(tokens.shape, BF16)] * 2 + [pltpu.VMEM((count, LANES), BF16)],
        in_specs=[hbm] * len(args),
        out_specs=[vm] * 3,
        scratch_shapes=list(sc.values())
        + [pltpu.VMEM(a.shape, a.dtype) for a in args]
        + [
            pltpu.SemaphoreType.DMA((len(args),)),
            pltpu.VMEM((count, LANES), BF16),
            pltpu.VMEM((LAST, D), F32),
            pltpu.SemaphoreType.DMA((sems,)),
            pltpu.SemaphoreType.DMA((sems,)),
        ]
        + shapes,
        compiler_params=params,
        name="blocks",
    )(*args)
    weights = (pos_t, again, abias, qkv, lepe_t, proj, mgain, mbias, fc1, fc2)
    shapes = [jax.ShapeDtypeStruct(tokens.shape, BF16)] * 2 + [jax.ShapeDtypeStruct(w.shape, F32) for w in weights]
    res = pl.pallas_call(
        partial(finish_body, layers),
        out_shape=shapes,
        in_specs=[vm] * 3,
        out_specs=[hbm] * 12,
        scratch_shapes=[pltpu.VMEM(a.shape, a.dtype) for a in shapes] + [pltpu.SemaphoreType.DMA((2 + 4 * layers + 6,))],
        compiler_params=pltpu.CompilerParams(vmem_limit_bytes=32 * 2**20),
        name="widen",
    )(total, out, gin)
    res = list(res)
    res[2] = jnp.transpose(res[2], (1, 0, 2))
    res[6] = jnp.transpose(res[6], (1, 0, 2))
    return tuple(res)


def solution(mesh):
    image = P("section", "dp", None, None)
    sections, dps = mesh.shape["section"], mesh.shape["dp"]
    return jax.shard_map(
        partial(per_device, sections, dps),
        mesh=mesh,
        in_specs=(image, P("section", "dp", None, None, None, None)) + (P(),) * 10 + (image,),
        out_specs=(image, image) + (P(),) * 10,
        check_vma=False,
    )
```
